32 devices in a mesh: dp: 2 (over x), tm: 4 (over y, core), mp: 4 (over z).
Axes of the slice: x: 2, y: 2, z: 4, core: 2. Of those that a mesh axis runs over, the one named last changes fastest.
Arguments:
- activations: bfloat16 [2, 8, 5, 40, 1280], P('dp', 'tm', None, None, 'mp'), may hold values from -1200 to 1200
- norm_gain: float32 [1280], P('mp'), may hold values from 0.25 to 1.75
- norm_bias: float32 [1280], P('mp'), may hold values from -3 to 3
- spatial_weight: bfloat16 [9, 1280, 1280], P(None, 'mp', 'tm'), may hold values from -0.0546875 to 0.0546875
- temporal_weight: bfloat16 [3, 1280, 1280], P(None, 'tm', 'mp'), may hold values from -0.09375 to 0.09375
- cotangent: bfloat16 [2, 8, 5, 40, 1280], P('dp', 'tm', None, None, 'mp'), may hold values from -6 to 6
Outputs:
- block_output: bfloat16 [2, 8, 5, 40, 1280], P('dp', 'tm', None, None, 'mp')
- temporal_grad: float32 [3, 1280, 1280], P(None, 'tm', 'mp')
The draws below stay inside these ranges and needn't reach their ends.
All inputs are finite; a program needn't handle non-finite values.
Results may differ from the reference program's by a relative error of at most 0.0058.
Values may be sent and summed in bfloat16 or wider, within the bound.
No kernel may reach another device: no remote copies, remote signals or barrier semaphores. Data moves between devices by JAX's collectives and lax.ppermute only.
A program may use at most 64 MiB of HBM per device.

```python
import math
import jax
import jax.numpy as jnp
from jax import lax

CHANNELS = 1280
GROUPS = 32
ROWS_BAND = 5
COLUMNS = 40
FRAMES = 8
CLIPS = 2


def draw_activations(key, part):
    subkeys = jax.random.split(key, 3)
    shape = (CLIPS, FRAMES, ROWS_BAND, COLUMNS, CHANNELS)
    position_scale = jnp.exp(jax.random.uniform(subkeys[1], (CLIPS, FRAMES, ROWS_BAND, COLUMNS, 1), jnp.float32, 0.0, math.log(10.0)))
    channel_scale = jnp.exp(jax.random.uniform(subkeys[2], (CLIPS, 1, 1, 1, CHANNELS), jnp.float32, 0.0, math.log(10.0)))
    frame_index = jnp.arange(FRAMES, dtype=jnp.float32) / max(FRAMES - 1, 1)
    frame_scale = jnp.power(3.0, frame_index).reshape(1, FRAMES, 1, 1, 1)
    normal_part = jnp.clip(jax.random.normal(subkeys[0], shape, jnp.float32), -4.0, 4.0)
    values = normal_part * position_scale * channel_scale * frame_scale
    return values.astype(jnp.bfloat16)


def levels(own_key, shape, cuts, smallest, top_value):
    level = 1.0
    for axis_at, parts in cuts:
        draws = jax.random.uniform(jax.random.fold_in(jax.random.fold_in(own_key, 6), axis_at), (parts,), jnp.float32, smallest / len(cuts), top_value / len(cuts))
        level = level * jnp.repeat(jnp.exp(draws), shape[axis_at] // parts).reshape((-1,) + (1,) * (len(shape) - 1 - axis_at))
    return level


def scatter_about(rng, shape, scale, bound, cuts=(), held_as=jnp.bfloat16):
    drawn = scale * jax.random.normal(rng, shape, jnp.float32)
    if cuts:
        drawn = drawn * levels(rng, shape, cuts, -0.22, 0.18)
    return jnp.clip(drawn, -bound, bound).astype(held_as)


def setup_inputs(seed: int = 0) -> dict:
    key_of = jax.random.split(jax.random.key(seed), 7)
    return {
        "activations": draw_activations(jax.random.fold_in(key_of[6], 71), 0),
        "norm_gain": jnp.clip(1.0 + 0.15 * jax.random.normal(key_of[1], (CHANNELS,), jnp.float32), 0.25, 1.75),
        "norm_bias": scatter_about(key_of[2], (CHANNELS,), 0.5, 3.0, ((0, 4),), jnp.float32),
        "spatial_weight": scatter_about(key_of[3], (9, CHANNELS, CHANNELS), (9 * CHANNELS) ** -0.5, 0.0546875, ((1, 4), (2, 4))),
        "temporal_weight": scatter_about(key_of[4], (3, CHANNELS, CHANNELS), (3 * CHANNELS) ** -0.5, 0.09375, ((1, 4), (2, 4))),
        "cotangent": scatter_about(key_of[5], (CLIPS, FRAMES, ROWS_BAND, COLUMNS, CHANNELS), 1.0, 6.0, ((0, 2), (1, 4), (4, 4))),
    }


epsilon = 1e-05

def group_silu(clip_values, norm_gain, norm_bias):
    values = clip_values.astype(jnp.float32)
    shaped = values.reshape(values.shape[:3] + (GROUPS, CHANNELS // GROUPS))
    average = lax.optimization_barrier(jnp.mean(shaped, axis=(0, 1, 2, 4), keepdims=True))
    centered = shaped - average
    variance = lax.optimization_barrier(jnp.mean(centered * centered, axis=(0, 1, 2, 4), keepdims=True))
    normed = (centered * lax.rsqrt(variance + epsilon)).reshape(values.shape) * norm_gain + norm_bias
    return jax.nn.silu(normed).astype(jnp.bfloat16)

def spatial_conv(hidden, spatial_weight):
    padded = jnp.pad(hidden, ((0, 0), (1, 1), (1, 1), (0, 0)))
    summed = jnp.zeros((FRAMES * ROWS_BAND * COLUMNS, CHANNELS), jnp.float32)
    for tap_index in range(9):
        row_shift = tap_index // 3
        col_shift = tap_index % 3
        window = padded[:, row_shift:row_shift + ROWS_BAND, col_shift:col_shift + COLUMNS, :].reshape(-1, CHANNELS)
        summed = summed + jnp.dot(window, spatial_weight[tap_index], preferred_element_type=jnp.float32)
    return summed.reshape(FRAMES, ROWS_BAND, COLUMNS, CHANNELS).astype(jnp.bfloat16)

def reference(activations, norm_gain, norm_bias, spatial_weight, temporal_weight, cotangent):

    def per_clip(running, clip_pair):
        clip_values, clip_grad = clip_pair
        hidden = group_silu(clip_values, norm_gain, norm_bias)
        spatial = spatial_conv(hidden, spatial_weight)
        spatial_pad = jnp.pad(spatial, ((1, 1), (0, 0), (0, 0), (0, 0)))
        summed = jnp.zeros((FRAMES * ROWS_BAND * COLUMNS, CHANNELS), jnp.float32)
        flat_grad = clip_grad.reshape(-1, CHANNELS)
        tap_terms = []
        for tap_index in range(3):
            window = spatial_pad[tap_index:tap_index + FRAMES].reshape(-1, CHANNELS)
            summed = summed + jnp.dot(window, temporal_weight[tap_index], preferred_element_type=jnp.float32)
            tap_terms.append(lax.dot_general(window, flat_grad, (((0,), (0,)), ((), ())), preferred_element_type=jnp.float32))
        produced = summed.reshape(FRAMES, ROWS_BAND, COLUMNS, CHANNELS).astype(jnp.bfloat16)
        return (running + jnp.stack(tap_terms), produced)
    start_value = jnp.zeros((3, CHANNELS, CHANNELS), jnp.float32)
    grad_total, outputs = lax.scan(per_clip, start_value, (activations, cotangent))
    return (outputs, grad_total / CLIPS)
```

```python
import functools

import jax
import jax.numpy as jnp
from jax import lax
from jax.experimental import pallas as pl
from jax.experimental.pallas import tpu as pltpu
from jax.sharding import PartitionSpec as P

CHANNELS = 1280
GROUPS = 32
GROUP_WIDTH = CHANNELS // GROUPS
EPSILON = 1e-05

f32 = jnp.float32
bf16 = jnp.bfloat16


def group_sum(rows):
    width = rows.shape[1]
    first = lax.broadcasted_iota(jnp.int32, (width, width), 0) // GROUP_WIDTH
    second = lax.broadcasted_iota(jnp.int32, (width, width), 1) // GROUP_WIDTH
    same = jnp.where(first == second, 1.0, 0.0).astype(f32)
    return jnp.dot(rows, same, precision=lax.Precision.HIGHEST, preferred_element_type=f32)


def stats_kernel(x_ref, out_ref):
    frames, rows, cols, width = x_ref.shape
    count = frames * rows * cols
    values = x_ref[...].astype(f32).reshape(count // 8, 8, width)
    mean = group_sum(values.sum(axis=0)).sum(axis=0, keepdims=True) / (count * GROUP_WIDTH)
    centered = values - mean[None]
    square = group_sum((centered * centered).sum(axis=0)).sum(axis=0, keepdims=True)
    out_ref[0:8, :] = jnp.broadcast_to(mean, (8, width))
    out_ref[8:16, :] = jnp.broadcast_to(square, (8, width))


def piece_stats(piece):
    return pl.pallas_call(
        stats_kernel,
        out_shape=jax.ShapeDtypeStruct((16, piece.shape[-1]), f32),
        in_specs=[pl.BlockSpec(memory_space=pltpu.VMEM)],
        out_specs=pl.BlockSpec(memory_space=pltpu.VMEM),
        name="piece_stats",
    )(piece)


def conv_kernel(x_ref, s0_ref, s1_ref, s2_ref, s3_ref, gain_ref, bias_ref, w_ref, out_ref, cols_ref):
    frames, rows, cols, width = x_ref.shape
    band = frames * cols
    stats = [s0_ref, s1_ref, s2_ref, s3_ref]
    means = [s[0:8, :] for s in stats]
    mean = (means[0] + means[1] + means[2] + means[3]) / 4.0
    count = frames * rows * cols * GROUP_WIDTH
    square = sum(s[8:16, :] for s in stats)
    square = square + count * sum((m - mean) * (m - mean) for m in means)
    scale = lax.rsqrt(square / (4.0 * count) + EPSILON)[0:1]
    mean = mean[0:1]
    gain = gain_ref[...]
    bias = bias_ref[...]
    cols_ref[0:band, :] = jnp.zeros((band, 3 * width), bf16)
    cols_ref[(rows + 1) * band :, :] = jnp.zeros((band, 3 * width), bf16)
    column = lax.broadcasted_iota(jnp.int32, (band, width), 0) % cols
    for row in range(rows):
        values = jnp.concatenate([x_ref[f, row].astype(f32) for f in range(frames)], axis=0)
        normed = (values - mean) * scale * gain + bias
        hidden = normed / (1.0 + jnp.exp(-normed))
        left = jnp.where(column == 0, 0.0, pltpu.roll(hidden, 1, 0))
        right = jnp.where(column == cols - 1, 0.0, pltpu.roll(hidden, band - 1, 0))
        line = jnp.concatenate([left.astype(bf16), hidden.astype(bf16), right.astype(bf16)], axis=1)
        cols_ref[(row + 1) * band : (row + 2) * band, :] = line
    total = jnp.dot(cols_ref[0 : rows * band, :], w_ref[0], preferred_element_type=f32)
    for tap in (1, 2):
        total = total + jnp.dot(
            cols_ref[tap * band : (tap + rows) * band, :], w_ref[tap], preferred_element_type=f32
        )
    out_ref[...] = total.astype(bf16)


def piece_conv(piece, stats, gain, bias, weight):
    frames, rows, cols, width = piece.shape
    width_out = weight.shape[-1]
    count = frames * rows * cols
    return pl.pallas_call(
        conv_kernel,
        out_shape=jax.ShapeDtypeStruct((count, width_out), bf16),
        in_specs=[pl.BlockSpec(memory_space=pltpu.VMEM)] * 8,
        out_specs=pl.BlockSpec(memory_space=pltpu.VMEM),
        scratch_shapes=[pltpu.VMEM(((rows + 2) * frames * cols, 3 * width), bf16)],
        compiler_params=pltpu.CompilerParams(vmem_limit_bytes=32 * 1024 * 1024),
        cost_estimate=pl.CostEstimate(
            flops=2 * count * 9 * width * width_out,
            bytes_accessed=2 * 9 * width * width_out + 4 * count * width,
            transcendentals=count * width,
        ),
        name="piece_conv",
    )(piece, *stats, gain, bias, weight)


def xor(axis_size, bit):
    return [(i, i ^ bit) for i in range(axis_size)]


def add16(a, b):
    return (a.astype(f32) + b.astype(f32)).astype(bf16)


def tie(x, *others):
    return lax.optimization_barrier((x,) + others)[0]


def line_all_reduce(parts):
    position = lax.axis_index("mp")
    at_end = (position == 0) | (position == 3)
    n = len(parts)
    arrived = [lax.ppermute(p, "mp", [(0, 1), (3, 2)]) for p in parts]
    half, other, full, back, out = ([None] * n for _ in range(5))
    last = parts[0]
    for k in range(n + 2):
        if k < n:
            half[k] = add16(tie(parts[k], last), arrived[k])
            other[k] = lax.ppermute(half[k], "mp", [(1, 2), (2, 1)])
            last = half[k]
        if 0 <= k - 1 < n:
            full[k - 1] = add16(tie(half[k - 1], last), other[k - 1])
            back[k - 1] = lax.ppermute(full[k - 1], "mp", [(1, 0), (2, 3)])
            last = full[k - 1]
        if 0 <= k - 2 < n:
            out[k - 2] = jnp.where(at_end, back[k - 2], tie(full[k - 2], last))
            last = out[k - 2]
    return out


def in_order(pieces):
    index = lax.axis_index("tm")
    odd = (index & 1) == 1
    high = (index & 2) == 2
    a, b, c, d = pieces
    a, b = jnp.where(odd, b, a), jnp.where(odd, a, b)
    c, d = jnp.where(odd, d, c), jnp.where(odd, c, d)
    a, c = jnp.where(high, c, a), jnp.where(high, a, c)
    b, d = jnp.where(high, d, b), jnp.where(high, b, d)
    return jnp.concatenate([a, b, c, d], axis=0)


def body(activations, norm_gain, norm_bias, spatial_weight, temporal_weight, cotangent):
    own = activations[0]
    frames, rows, cols, width = own.shape
    width_out = spatial_weight.shape[2]
    core, chip = xor(4, 1), xor(4, 2)
    count = rows * cols

    st_own = piece_stats(own)
    st_chip = lax.ppermute(st_own, "tm", chip)
    st_core = lax.ppermute(st_own, "tm", core)
    st_both = lax.ppermute(st_own, "tm", xor(4, 3))
    raw_core = lax.ppermute(own, "tm", core)
    raw_chip = lax.ppermute(own, "tm", chip)
    raw_both = lax.ppermute(raw_chip, "tm", core)
    stats = (st_own, st_core, st_chip, st_both)

    gain = norm_gain.reshape(1, width)
    bias = norm_bias.reshape(1, width)
    taps = spatial_weight.reshape(3, 3 * width, width_out)
    parts = []
    for piece in (own, raw_core, raw_chip, raw_both):
        parts.append(piece_conv(piece, stats, gain, bias, taps))
    reduced = line_all_reduce(parts)

    cot_own = cotangent[0]
    cot_core = lax.ppermute(cot_own, "tm", core)
    cot_chip = lax.ppermute(cot_own, "tm", chip)
    cot_both = lax.ppermute(cot_chip, "tm", core)
    cot = in_order([cot_own, cot_core, cot_chip, cot_both]).reshape(-1, cot_own.shape[-1])

    spatial = in_order(
        [r.reshape(rows, frames, cols, width_out).transpose(1, 0, 2, 3) for r in reduced]
    )
    frames_all = 4 * frames
    padded = jnp.pad(spatial, ((1, 1), (0, 0), (0, 0), (0, 0)))
    windows = [padded[k : k + frames_all].reshape(-1, width_out) for k in range(3)]

    clips = lax.axis_size("dp")
    grads = []
    for k in range(3):
        grads.append(
            lax.dot_general(
                windows[k], cot, (((0,), (0,)), ((), ())), preferred_element_type=f32
            )
        )
    grad = jnp.stack(grads)
    if clips == 2:
        sent = grad.astype(bf16)
        other = lax.ppermute(sent, "dp", [(0, 1), (1, 0)])
        temporal_grad = (sent.astype(f32) + other.astype(f32)) / clips
    else:
        temporal_grad = lax.psum(grad, "dp") / clips

    summed = sum(
        jnp.dot(windows[k], temporal_weight[k], preferred_element_type=f32) for k in range(3)
    ).reshape(4, frames, rows, cols, -1)
    index = lax.axis_index("tm")
    part = [lax.dynamic_index_in_dim(summed, index ^ i, 0, keepdims=False) for i in range(4)]
    far = lax.ppermute(part[3].astype(bf16), "tm", core)
    near = lax.ppermute(part[1].astype(bf16), "tm", core)
    to_chip = (part[2] + far.astype(f32)).astype(bf16)
    from_chip = lax.ppermute(to_chip, "tm", chip)
    block = (part[0] + near.astype(f32) + from_chip.astype(f32)).astype(bf16)[None]
    return block, temporal_grad


def solution(mesh):
    in_specs = (
        P("dp", "tm", None, None, "mp"),
        P("mp"),
        P("mp"),
        P(None, "mp", "tm"),
        P(None, "tm", "mp"),
        P("dp", "tm", None, None, "mp"),
    )
    out_specs = (P("dp", "tm", None, None, "mp"), P(None, "tm", "mp"))
    return jax.shard_map(body, mesh=mesh, in_specs=in_specs, out_specs=out_specs, check_vma=False)
```

```python
import functools

import jax
import jax.numpy as jnp
from jax import lax
from jax.experimental import pallas as pl
from jax.experimental.pallas import tpu as pltpu
from jax.sharding import PartitionSpec as P

CHANNELS = 1280
GROUPS = 32
GROUP_WIDTH = CHANNELS // GROUPS
EPSILON = 1e-05

f32 = jnp.float32
bf16 = jnp.bfloat16


def group_sum(rows):
    width = rows.shape[1]
    first = lax.broadcasted_iota(jnp.int32, (width, width), 0) // GROUP_WIDTH
    second = lax.broadcasted_iota(jnp.int32, (width, width), 1) // GROUP_WIDTH
    same = jnp.where(first == second, 1.0, 0.0).astype(f32)
    return jnp.dot(rows, same, precision=lax.Precision.HIGHEST, preferred_element_type=f32)


def stats_kernel(x_ref, out_ref):
    frames, rows, cols, width = x_ref.shape
    count = frames * rows * cols
    values = x_ref[...].astype(f32).reshape(count // 8, 8, width)
    mean = group_sum(values.sum(axis=0)).sum(axis=0, keepdims=True) / (count * GROUP_WIDTH)
    centered = values - mean[None]
    square = group_sum((centered * centered).sum(axis=0)).sum(axis=0, keepdims=True)
    out_ref[0:8, :] = jnp.broadcast_to(mean, (8, width))
    out_ref[8:16, :] = jnp.broadcast_to(square, (8, width))


def vmem_spec():
    return pl.BlockSpec(memory_space=pltpu.VMEM)


def params(mebibytes):
    return pltpu.CompilerParams(vmem_limit_bytes=mebibytes * 1024 * 1024)


def piece_stats(piece):
    return pl.pallas_call(
        stats_kernel,
        out_shape=jax.ShapeDtypeStruct((16, piece.shape[-1]), f32),
        in_specs=[vmem_spec()],
        out_specs=vmem_spec(),
        compiler_params=params(6),
        name="piece_stats",
    )(piece)


def conv_kernel(x_ref, s0_ref, s1_ref, s2_ref, s3_ref, gain_ref, bias_ref, w_ref, keep_ref, send_ref, cols_ref):
    frames, rows, cols, width = x_ref.shape
    band = frames * cols
    stats = [s0_ref, s1_ref, s2_ref, s3_ref]
    means = [s[0:8, :] for s in stats]
    mean = (means[0] + means[1] + means[2] + means[3]) / 4.0
    count = frames * rows * cols * GROUP_WIDTH
    square = sum(s[8:16, :] for s in stats)
    square = square + count * sum((m - mean) * (m - mean) for m in means)
    scale = lax.rsqrt(square / (4.0 * count) + EPSILON)[0:1]
    mean = mean[0:1]
    gain = gain_ref[...].reshape(1, width)
    bias = bias_ref[...].reshape(1, width)
    cols_ref[0:band, :] = jnp.zeros((band, 3 * width), bf16)
    cols_ref[(rows + 1) * band :, :] = jnp.zeros((band, 3 * width), bf16)
    column = lax.broadcasted_iota(jnp.int32, (band, width), 0) % cols
    for row in range(rows):
        values = jnp.concatenate([x_ref[f, row].astype(f32) for f in range(frames)], axis=0)
        normed = (values - mean) * scale * gain + bias
        hidden = normed / (1.0 + jnp.exp(-normed))
        left = jnp.where(column == 0, 0.0, pltpu.roll(hidden, 1, 0))
        right = jnp.where(column == cols - 1, 0.0, pltpu.roll(hidden, band - 1, 0))
        line = jnp.concatenate([left.astype(bf16), hidden.astype(bf16), right.astype(bf16)], axis=1)
        cols_ref[(row + 1) * band : (row + 2) * band, :] = line
    total = jnp.dot(cols_ref[0 : rows * band, :], w_ref[0], preferred_element_type=f32)
    for tap in (1, 2):
        total = total + jnp.dot(
            cols_ref[tap * band : (tap + rows) * band, :], w_ref[tap], preferred_element_type=f32
        )
    total = total.reshape(rows, frames, cols, total.shape[-1])
    half = frames // 2
    low = total[:, :half].reshape(rows, half * cols, -1)
    high = total[:, half:].reshape(rows, half * cols, -1)
    odd = lax.axis_index("mp") % 2

    @pl.when(odd == 0)
    def _():
        keep_ref[...] = low.reshape(keep_ref.shape)
        send_ref[...] = high.reshape(keep_ref.shape).astype(bf16)

    @pl.when(odd == 1)
    def _():
        keep_ref[...] = high.reshape(keep_ref.shape)
        send_ref[...] = low.reshape(keep_ref.shape).astype(bf16)


def piece_conv(piece, stats, gain, bias, weight):
    frames, rows, cols, width = piece.shape
    width_out = weight.shape[-1]
    count = frames * rows * cols
    return pl.pallas_call(
        conv_kernel,
        out_shape=(
            jax.ShapeDtypeStruct((count // 2, width_out), f32),
            jax.ShapeDtypeStruct((count // 2, width_out), bf16),
        ),
        in_specs=[vmem_spec()] * 8,
        out_specs=(vmem_spec(), vmem_spec()),
        scratch_shapes=[pltpu.VMEM(((rows + 2) * frames * cols, 3 * width), bf16)],
        compiler_params=params(14),
        cost_estimate=pl.CostEstimate(
            flops=2 * count * 9 * width * width_out,
            bytes_accessed=2 * 9 * width * width_out + 4 * count * width,
            transcendentals=count * width,
        ),
        name="piece_conv",
    )(piece, *stats, gain, bias, weight)


PAD = 8


def fill_frames(scratch, mine, other):
    tm = lax.axis_index("tm")
    odd = lax.axis_index("mp") % 2
    frames, rows, width = scratch.shape
    scratch[0] = jnp.zeros((rows, width), bf16)
    scratch[frames - 1] = jnp.zeros((rows, width), bf16)
    for i in range(4):
        block = 1 + 2 * jnp.bitwise_xor(tm, i)
        scratch[block + odd, 0 : rows - PAD] = mine[i][...]
        scratch[block + 1 - odd, 0 : rows - PAD] = other[i][...]
    for f in range(1, frames - 1):
        scratch[f, rows - PAD :] = jnp.zeros((PAD, width), bf16)


def grad_kernel(m0, m1, m2, m3, o0, o1, o2, o3, c0, c1, c2, c3, out_ref, s_ref, c_ref):
    fill_frames(s_ref, [m0, m1, m2, m3], [o0, o1, o2, o3])
    tm = lax.axis_index("tm")
    frames, rows, width = c_ref.shape
    for i, c in enumerate((c0, c1, c2, c3)):
        block = 2 * jnp.bitwise_xor(tm, i)
        for f in range(2):
            c_ref[block + f, 0 : rows - PAD] = c[f]
    for f in range(frames):
        c_ref[f, rows - PAD :] = jnp.zeros((PAD, width), bf16)
    cot = c_ref[...].reshape(frames * rows, width)
    for k in range(3):
        window = s_ref[k : k + frames].reshape(frames * rows, s_ref.shape[-1])
        out_ref[k] = lax.dot_general(
            window, cot, (((0,), (0,)), ((), ())), preferred_element_type=f32
        ).astype(out_ref.dtype)


def temporal_grads(mine, other, cot, dtype):
    count, width = mine[0].shape
    width_out = cot[0].shape[-1]
    return pl.pallas_call(
        grad_kernel,
        out_shape=jax.ShapeDtypeStruct((3, width, width_out), dtype),
        in_specs=[vmem_spec()] * 12,
        out_specs=vmem_spec(),
        scratch_shapes=[
            pltpu.VMEM((10, count + PAD, width), bf16),
            pltpu.VMEM((8, count + PAD, width_out), bf16),
        ],
        compiler_params=params(20),
        cost_estimate=pl.CostEstimate(
            flops=2 * 3 * 8 * count * width * width_out,
            bytes_accessed=4 * 8 * count * width,
            transcendentals=0,
        ),
        name="temporal_grads",
    )(*mine, *other, *cot)


def temporal_kernel(blocks, m0, m1, m2, m3, o0, o1, o2, o3, w_ref, send_ref, keep_ref, s_ref):
    fill_frames(s_ref, [m0, m1, m2, m3], [o0, o1, o2, o3])
    tm = lax.axis_index("tm")
    frames, rows, width = s_ref.shape
    for i, out in zip(blocks, (send_ref, keep_ref), strict=True):
        first = 2 * jnp.bitwise_xor(tm, i)
        total = None
        for k in range(3):
            window = s_ref[pl.ds(first + k, 2)].reshape(2 * rows, width)
            term = jnp.dot(window, w_ref[k], preferred_element_type=f32)
            total = term if total is None else total + term
        total = total.reshape(2, rows, -1)[:, : rows - PAD]
        out[...] = total.astype(out.dtype)


def temporal_conv(blocks, mine, other, weight):
    count, width = mine[0].shape
    width_out = weight.shape[-1]
    return pl.pallas_call(
        functools.partial(temporal_kernel, blocks),
        out_shape=(
            jax.ShapeDtypeStruct((2, count, width_out), bf16),
            jax.ShapeDtypeStruct((2, count, width_out), f32),
        ),
        in_specs=[vmem_spec()] * 9,
        out_specs=(vmem_spec(), vmem_spec()),
        scratch_shapes=[pltpu.VMEM((10, count + PAD, width), bf16)],
        compiler_params=params(16),
        cost_estimate=pl.CostEstimate(
            flops=2 * 3 * 4 * count * width * width_out,
            bytes_accessed=4 * 8 * count * width,
            transcendentals=0,
        ),
        name="temporal_conv",
    )(*mine, *other, weight)


def xor(axis_size, bit):
    return [(i, i ^ bit) for i in range(axis_size)]


def add16(a, b):
    return (a.astype(f32) + b.astype(f32)).astype(bf16)


def tie(x, *others):
    return lax.optimization_barrier((x,) + others)[0]


def body(activations, norm_gain, norm_bias, spatial_weight, temporal_weight, cotangent):
    own = activations[0]
    frames, rows, cols, width = own.shape
    width_out = spatial_weight.shape[2]
    core, chip = xor(4, 1), xor(4, 2)
    near, far = xor(4, 1), xor(4, 2)
    count = rows * cols

    raw_core = lax.ppermute(own, "tm", core)
    raw_chip = lax.ppermute(own, "tm", chip)
    st_own = piece_stats(own)
    st_chip = lax.ppermute(st_own, "tm", chip)
    st_core = lax.ppermute(st_own, "tm", core)
    st_both = lax.ppermute(st_own, "tm", xor(4, 3))
    raw_both = lax.ppermute(raw_chip, "tm", core)
    stats = (st_own, st_core, st_chip, st_both)
    taps = spatial_weight.reshape(3, 3 * width, width_out)

    pieces = (own, raw_core, raw_chip, raw_both)
    keep, got, part, across, mine, other = ([None] * 4 for _ in range(6))
    last = None
    for step, i in ("c0", "c1", "c2", "s0", "c3", "s1", "f0", "s2", "f1", "s3", "f2", "f3"):
        i = int(i)
        if step == "c":
            piece = pieces[i] if last is None else tie(pieces[i], last)
            keep[i], send = piece_conv(piece, stats, norm_gain, norm_bias, taps)
            got[i] = lax.ppermute(send, "mp", near)
            last = keep[i]
        elif step == "s":
            part[i] = add16(tie(keep[i], last), got[i])
            across[i] = lax.ppermute(part[i], "mp", far)
            last = part[i]
        else:
            mine[i] = add16(tie(part[i], last), across[i])
            other[i] = lax.ppermute(mine[i], "mp", near)
            last = mine[i]

    cot_own = tie(cotangent[0].reshape(frames, count, width), part[1])
    cot_core = lax.ppermute(cot_own, "tm", core)
    cot_chip = lax.ppermute(cot_own, "tm", chip)
    cot_both = lax.ppermute(cot_chip, "tm", core)
    cot = (cot_own, cot_core, cot_chip, cot_both)

    clips = lax.axis_size("dp")
    if clips == 2:
        sent = temporal_grads(mine, other, cot, bf16)
        theirs = lax.ppermute(sent, "dp", [(0, 1), (1, 0)])
        temporal_grad = (sent.astype(f32) + theirs.astype(f32)) / clips
    else:
        sent = temporal_grads(mine, other, cot, f32)
        temporal_grad = lax.psum(sent, "dp") / clips

    send, keep_chip = temporal_conv((3, 2), [tie(mine[0], sent)] + mine[1:], other, temporal_weight)
    far_part = lax.ppermute(send, "tm", core)
    send, keep_own = temporal_conv((1, 0), [tie(mine[0], send)] + mine[1:], other, temporal_weight)
    near_part = lax.ppermute(send, "tm", core)
    from_chip = lax.ppermute(add16(keep_chip, far_part), "tm", chip)
    block = (keep_own + near_part.astype(f32) + from_chip.astype(f32)).astype(bf16)
    return block.reshape(activations.shape), temporal_grad


def solution(mesh):
    in_specs = (
        P("dp", "tm", None, None, "mp"),
        P("mp"),
        P("mp"),
        P(None, "mp", "tm"),
        P(None, "tm", "mp"),
        P("dp", "tm", None, None, "mp"),
    )
    out_specs = (P("dp", "tm", None, None, "mp"), P(None, "tm", "mp"))
    return jax.shard_map(body, mesh=mesh, in_specs=in_specs, out_specs=out_specs, check_vma=False)
```

```python
import functools

import jax
import jax.numpy as jnp
from jax import lax
from jax.experimental import pallas as pl
from jax.experimental.pallas import tpu as pltpu
from jax.sharding import PartitionSpec as P

CHANNELS = 1280
GROUPS = 32
GROUP_WIDTH = CHANNELS // GROUPS
EPSILON = 1e-05


def cost(microseconds):
    return pl.CostEstimate(flops=int(microseconds * 1.15e9), bytes_accessed=1, transcendentals=0)


f32 = jnp.float32
bf16 = jnp.bfloat16


def group_sum(rows):
    width = rows.shape[1]
    first = lax.broadcasted_iota(jnp.int32, (width, width), 0) // GROUP_WIDTH
    second = lax.broadcasted_iota(jnp.int32, (width, width), 1) // GROUP_WIDTH
    same = jnp.where(first == second, 1.0, 0.0).astype(f32)
    return jnp.dot(rows, same, precision=lax.Precision.HIGHEST, preferred_element_type=f32)


def vmem_spec():
    return pl.BlockSpec(memory_space=pltpu.VMEM)


def any_spec():
    return pl.BlockSpec(memory_space=pltpu.HBM)


def params(mebibytes):
    return pltpu.CompilerParams(vmem_limit_bytes=mebibytes * 1024 * 1024)


def stats_kernel(own_ref, core_ref, stats_ref, frames_ref):
    core = lax.axis_index("tm") % 2
    frames_ref[core] = own_ref[...]
    frames_ref[1 - core] = core_ref[...]
    width = frames_ref.shape[-1]
    values = [ref[...].astype(f32).reshape(-1, 8, width) for ref in (own_ref, core_ref)]
    mean, square = moments(jnp.concatenate(values, axis=0))
    stats_ref[0:8, :] = jnp.broadcast_to(mean, (8, width))
    stats_ref[8:16, :] = jnp.broadcast_to(square, (8, width))


def chip_stats(own, sibling):
    width = own.shape[-1]
    return pl.pallas_call(
        stats_kernel,
        out_shape=(
            jax.ShapeDtypeStruct((16, width), f32),
            jax.ShapeDtypeStruct((2,) + own.shape, bf16),
        ),
        in_specs=[vmem_spec()] * 2,
        out_specs=(vmem_spec(),) * 2,
        compiler_params=params(10),
        cost_estimate=cost(1.5),
        name="chip_stats",
    )(own, sibling)


def hold_kernel(w_ref, gain_ref, bias_ref, taps_ref, affine_ref, sem):
    copy = pltpu.make_async_copy(w_ref, taps_ref, sem)
    copy.start()
    width = gain_ref.shape[0]
    affine_ref[0:8, :] = jnp.broadcast_to(gain_ref[...].reshape(1, width), (8, width))
    affine_ref[8:16, :] = jnp.broadcast_to(bias_ref[...].reshape(1, width), (8, width))
    copy.wait()


def hold(taps, gain, bias):
    width = gain.shape[0]
    return pl.pallas_call(
        hold_kernel,
        out_shape=(
            jax.ShapeDtypeStruct(taps.shape, bf16),
            jax.ShapeDtypeStruct((16, width), f32),
        ),
        in_specs=[any_spec(), vmem_spec(), vmem_spec()],
        out_specs=(vmem_spec(),) * 2,
        scratch_shapes=[pltpu.SemaphoreType.DMA],
        compiler_params=params(4),
        cost_estimate=cost(1.0),
        name="hold_weights",
    )(taps, gain, bias)


def moments(values):
    count = values.shape[0] * 8 * GROUP_WIDTH
    mean = group_sum(values.sum(axis=0)).sum(axis=0, keepdims=True) / count
    centered = values - mean[None]
    square = group_sum((centered * centered).sum(axis=0)).sum(axis=0, keepdims=True)
    return mean, square


def held_half():
    z = lax.axis_index("mp")
    return (z + z // 2) % 2


def conv_kernel(x_ref, norm_ref, w_ref, keep_ref, send_ref, cols_ref):
    n, frames, rows, cols, width = x_ref.shape
    band = frames * cols
    odd = held_half()
    mean, scale = norm_ref[0:1, :], norm_ref[8:9, :]
    gain, bias = norm_ref[16:17, :], norm_ref[24:25, :]
    column = lax.broadcasted_iota(jnp.int32, (band, width), 0) % cols
    size = keep_ref.shape[0] // n
    for j in range(n):
        cols_ref[j, 0:band, :] = jnp.zeros((band, 3 * width), bf16)
        cols_ref[j, (rows + 1) * band :, :] = jnp.zeros((band, 3 * width), bf16)
        for row in range(rows):
            values = jnp.concatenate([x_ref[j, f, row].astype(f32) for f in range(frames)], axis=0)
            normed = (values - mean) * scale * gain + bias
            hidden = normed / (1.0 + jnp.exp(-normed))
            left = jnp.where(column == 0, 0.0, pltpu.roll(hidden, 1, 0))
            right = jnp.where(column == cols - 1, 0.0, pltpu.roll(hidden, band - 1, 0))
            line = [left.astype(bf16), hidden.astype(bf16), right.astype(bf16)]
            cols_ref[j, (row + 1) * band : (row + 2) * band, :] = jnp.concatenate(line, axis=1)
        total = None
        for tap in range(3):
            window = cols_ref[j, tap * band : (tap + rows) * band, :]
            term = jnp.dot(window, w_ref[tap], preferred_element_type=f32)
            total = term if total is None else total + term
        total = total.reshape(rows, frames, cols, total.shape[-1])
        half = frames // 2
        low = total[:, :half].reshape(size, -1)
        high = total[:, half:].reshape(size, -1)
        here = slice(j * size, (j + 1) * size)

        @pl.when(odd == 0)
        def _():
            keep_ref[here] = low
            send_ref[here] = high.astype(bf16)

        @pl.when(odd == 1)
        def _():
            keep_ref[here] = high
            send_ref[here] = low.astype(bf16)


def pair_conv(pairs, norm, taps, weight):
    n, frames, rows, cols, width = pairs.shape
    width_out = taps.shape[-1]
    count = n * frames * rows * cols // 2
    return pl.pallas_call(
        conv_kernel,
        out_shape=(
            jax.ShapeDtypeStruct((count, width_out), f32),
            jax.ShapeDtypeStruct((count, width_out), bf16),
        ),
        in_specs=[vmem_spec()] * 3,
        out_specs=(vmem_spec(),) * 2,
        scratch_shapes=[pltpu.VMEM((n, (rows + 2) * frames * cols, 3 * width), bf16)],
        compiler_params=params(20),
        cost_estimate=cost(weight),
        name="pair_conv",
    )(pairs, norm, taps)


PAD = 8

CLAIM = {
    "merge": 50.0,
    "conv0": 50.0,
    "collect": 0.01,
    "part": 0.01,
    "part0": 80.0,
    "conv1": 1.0,
    "mine": 50.0,
    "t1": 0.01,
    "g1": 0.01,
    "t2": 0.01,
    "g2": 50.0,
}


def pair_of(step):
    t = lax.axis_index("tm")
    return (t - t % 2, t - t % 2 + 1, jnp.bitwise_xor(t, 2), jnp.bitwise_xor(t, 3))[step]


def zero_frames(ref, lead, count, rows, width):
    ref[lead + (0,)] = jnp.zeros((rows, width), bf16)
    ref[lead + (count - 1,)] = jnp.zeros((rows, width), bf16)
    for f in range(1, count - 1):
        ref[lead + (f, slice(rows - PAD, rows))] = jnp.zeros((PAD, width), bf16)


def put_pairs(ref, lead, steps, pieces):
    odd = held_half()
    count = ref.shape[-2] - PAD
    steps = list(steps)
    for mine, other in zip(pieces[::2], pieces[1::2], strict=True):
        for j in range(mine.shape[0] // count):
            at = 1 + 2 * pair_of(steps.pop(0))
            ref[lead + (at + odd, slice(0, count))] = mine[j * count : (j + 1) * count]
            ref[lead + (at + 1 - odd, slice(0, count))] = other[j * count : (j + 1) * count]


def grad_kernel(steps, held, *refs):
    clips = refs[0].shape[0]
    cots, refs = refs[:4], refs[4:]
    *start, out_ref, s_ref, c_ref = refs[held * clips :]
    pieces = refs[: held * clips]
    t = lax.axis_index("tm")
    own = lax.axis_index("dp") if clips > 1 else 0
    frames, rows, width = s_ref.shape[1:]
    for clip in range(clips):
        at = own if clip == 0 else 1 - own
        zero_frames(s_ref, (at,), frames, rows, width)
        zero_frames(c_ref, (at,), frames, rows, c_ref.shape[-1])
        put_pairs(s_ref, (at,), steps, pieces[clip * held : (clip + 1) * held])
        for block, cot in enumerate(cots):
            first = 1 + 2 * jnp.bitwise_xor(t, block)
            for f in range(2):
                c_ref[at, first + f, 0 : rows - PAD] = cot[clip, f]
    chip = t // 2 if steps[0] == 0 else 1 - t // 2
    first, length = 1 + 4 * chip, 4
    turned = [
        s_ref[clip, pl.ds(first, length)].reshape(length * rows, width).T for clip in range(clips)
    ]
    for k in range(3):
        total = start[0][k] if start else None
        for clip in range(clips):
            cot = c_ref[clip, pl.ds(first + 1 - k, length)].reshape(length * rows, -1)
            term = jnp.dot(turned[clip], cot, preferred_element_type=f32)
            total = term if total is None else total + term
        out_ref[k] = total.astype(out_ref.dtype)


def temporal_grads(steps, cots, pieces, start, dtype, weight):
    clips, _, count, width_out = cots[0].shape
    width = pieces[0][0].shape[-1]
    held = len(pieces[0])
    operands = (*cots, *(p for clip in pieces for p in clip), *start)
    return pl.pallas_call(
        functools.partial(grad_kernel, steps, held),
        out_shape=jax.ShapeDtypeStruct((3, width, width_out), dtype),
        in_specs=[vmem_spec()] * len(operands),
        out_specs=vmem_spec(),
        scratch_shapes=[
            pltpu.VMEM((clips, 10, count + PAD, width), bf16),
            pltpu.VMEM((clips, 10, count + PAD, width_out), bf16),
        ],
        compiler_params=params(20),
        cost_estimate=cost(weight),
        name="temporal_grads",
    )(*operands)


def temporal_kernel(steps, blocks, *refs):
    *pieces, w_ref, send_ref, keep_ref, s_ref = refs
    frames, rows, width = s_ref.shape
    zero_frames(s_ref, (), frames, rows, width)
    put_pairs(s_ref, (), steps, pieces)
    for i, out in zip(blocks, (send_ref, keep_ref), strict=True):
        first = 2 * jnp.bitwise_xor(lax.axis_index("tm"), i)
        total = None
        for k in range(3):
            window = s_ref[pl.ds(first + k, 2)].reshape(2 * rows, width)
            term = jnp.dot(window, w_ref[k], preferred_element_type=f32)
            total = term if total is None else total + term
        total = total.reshape(2, rows, -1)[:, : rows - PAD]
        out[...] = total.astype(out.dtype)


def temporal_conv(steps, blocks, count, pieces, taps, weight):
    width, width_out = taps.shape[1:]
    return pl.pallas_call(
        functools.partial(temporal_kernel, steps, blocks),
        out_shape=(
            jax.ShapeDtypeStruct((2, count, width_out), bf16),
            jax.ShapeDtypeStruct((2, count, width_out), f32),
        ),
        in_specs=[vmem_spec()] * (len(pieces) + 1),
        out_specs=(vmem_spec(), vmem_spec()),
        scratch_shapes=[pltpu.VMEM((10, count + PAD, width), bf16)],
        compiler_params=params(16),
        cost_estimate=cost(weight),
        name="temporal_conv",
    )(*pieces, taps)


def xor(axis_size, bit):
    return [(i, i ^ bit) for i in range(axis_size)]


def add_kernel(a_ref, b_ref, out_ref):
    out_ref[...] = (a_ref[...].astype(f32) + b_ref[...].astype(f32)).astype(bf16)


def add16(a, b, weight):
    return pl.pallas_call(
        add_kernel,
        out_shape=jax.ShapeDtypeStruct(a.shape, bf16),
        in_specs=[vmem_spec()] * 2,
        out_specs=vmem_spec(),
        compiler_params=params(4),
        cost_estimate=cost(weight),
        name="add_parts",
    )(a, b)


def merge_kernel(s0_ref, s1_ref, affine_ref, out_ref, *, count):
    first, second = s0_ref[0:8, :], s1_ref[0:8, :]
    mean = (first + second) * 0.5
    square = s0_ref[8:16, :] + s1_ref[8:16, :]
    square = square + count * ((first - mean) * (first - mean) + (second - mean) * (second - mean))
    out_ref[0:8, :] = mean
    out_ref[8:16, :] = lax.rsqrt(square / (2.0 * count) + EPSILON)
    out_ref[16:32, :] = affine_ref[...]


def merge_stats(st_own, st_chip, affine, count, weight):
    return pl.pallas_call(
        functools.partial(merge_kernel, count=count),
        out_shape=jax.ShapeDtypeStruct((32, st_own.shape[1]), f32),
        in_specs=[vmem_spec()] * 3,
        out_specs=vmem_spec(),
        compiler_params=params(4),
        cost_estimate=cost(weight),
        name="merge_stats",
    )(st_own, st_chip, affine)


def collect_kernel(a_ref, b_ref, out_ref):
    out_ref[0] = a_ref[...]
    out_ref[1] = b_ref[...]


def collect(a, b, weight):
    return pl.pallas_call(
        collect_kernel,
        out_shape=jax.ShapeDtypeStruct((2,) + a.shape, a.dtype),
        in_specs=[vmem_spec()] * 2,
        out_specs=vmem_spec(),
        compiler_params=params(6),
        cost_estimate=cost(weight),
        name="collect_pairs",
    )(a, b)


def tie(x, *others):
    return lax.optimization_barrier((x,) + others)[0]


def body(activations, norm_gain, norm_bias, spatial_weight, temporal_weight, cotangent):
    own = activations[0]
    frames, rows, cols, width = own.shape
    width_out = spatial_weight.shape[2]
    core, chip = xor(4, 1), xor(4, 2)
    near, across = xor(4, 1), xor(4, 3)
    count = rows * cols
    clips = lax.axis_size("dp")
    sibling = lax.ppermute(own, "tm", core)
    st_own, pairs = chip_stats(own, sibling)
    st_chip = lax.ppermute(st_own, "tm", chip)
    taps, affine = hold(spatial_weight.reshape(3, 3 * width, width_out), norm_gain, norm_bias)
    raw_chip = lax.ppermute(tie(own, affine), "tm", chip)
    norm = merge_stats(st_own, st_chip, affine, 2 * frames * count * GROUP_WIDTH, CLAIM["merge"])

    keep0, send0 = pair_conv(pairs, norm, taps, CLAIM["conv0"])
    got0 = lax.ppermute(send0, "mp", near)
    raw_chip = tie(raw_chip, keep0)
    raw_both = lax.ppermute(raw_chip, "tm", core)
    far_pairs = collect(raw_chip, raw_both, CLAIM["collect"])
    part0 = add16(keep0, got0, CLAIM["part0"])
    came0 = lax.ppermute(part0, "mp", across)
    keep1, send1 = pair_conv(tie(far_pairs, part0), norm, taps, CLAIM["conv1"])
    got1 = lax.ppermute(send1, "mp", near)
    mine0 = add16(tie(part0, keep1), came0, CLAIM["mine"])
    part1 = add16(tie(keep1, mine0), got1, CLAIM["part"])
    came1 = lax.ppermute(part1, "mp", across)
    other0 = lax.ppermute(mine0, "mp", near)
    cot = cotangent.reshape(1, frames, count, width)
    cot_core = lax.ppermute(tie(cot, mine0), "tm", core)
    cot_chip = lax.ppermute(tie(cot, mine0), "tm", chip)
    mine1 = add16(tie(part1, mine0), came1, CLAIM["mine"])
    other1 = lax.ppermute(mine1, "mp", near)
    cot_both = lax.ppermute(tie(cot_chip, mine1), "tm", core)
    cots = (cot, cot_core, cot_chip, cot_both)

    steps = (0, 1, 2, 3)
    held = [tie(mine0, mine1), other0]
    grad = temporal_grads((0, 1), cots, [held], (), f32, CLAIM["g1"])
    sent = temporal_grads((2, 3), cots, [[mine1, other1]], (grad,), bf16 if clips == 2 else f32, CLAIM["g2"])
    pieces = [tie(mine0, sent), other0, mine1, other1]
    send, keep_chip = temporal_conv(steps, (3, 2), count, pieces, temporal_weight, CLAIM["t1"])
    far_part = lax.ppermute(send, "tm", core)
    later = [tie(mine0, keep_chip)] + pieces[1:]
    send, keep_own = temporal_conv(steps, (1, 0), count, later, temporal_weight, CLAIM["t2"])
    near_part = lax.ppermute(send, "tm", core)
    to_chip = add16(tie(keep_chip, keep_own), far_part, CLAIM["part"])
    from_chip = lax.ppermute(to_chip, "tm", chip)
    block = (keep_own + near_part.astype(f32) + from_chip.astype(f32)).astype(bf16)
    if clips == 2:
        theirs = lax.ppermute(sent, "dp", [(0, 1), (1, 0)])
        temporal_grad = (sent.astype(f32) + theirs.astype(f32)) / clips
    else:
        temporal_grad = lax.psum(sent, "dp") / clips
    return block.reshape(activations.shape), temporal_grad


def solution(mesh):
    in_specs = (
        P("dp", "tm", None, None, "mp"),
        P("mp"),
        P("mp"),
        P(None, "mp", "tm"),
        P(None, "tm", "mp"),
        P("dp", "tm", None, None, "mp"),
    )
    out_specs = (P("dp", "tm", None, None, "mp"), P(None, "tm", "mp"))
    return jax.shard_map(body, mesh=mesh, in_specs=in_specs, out_specs=out_specs, check_vma=False)
```

```python
import functools

import jax
import jax.numpy as jnp
from jax import lax
from jax.experimental import pallas as pl
from jax.experimental.pallas import tpu as pltpu
from jax.sharding import PartitionSpec as P

CHANNELS = 1280
GROUPS = 32
GROUP_WIDTH = CHANNELS // GROUPS
EPSILON = 1e-05


def cost(microseconds):
    return pl.CostEstimate(flops=int(microseconds * 1.15e9), bytes_accessed=1, transcendentals=0)


f32 = jnp.float32
bf16 = jnp.bfloat16


def group_sum(rows):
    width = rows.shape[1]
    first = lax.broadcasted_iota(jnp.int32, (width, width), 0) // GROUP_WIDTH
    second = lax.broadcasted_iota(jnp.int32, (width, width), 1) // GROUP_WIDTH
    same = jnp.where(first == second, 1.0, 0.0).astype(f32)
    return jnp.dot(rows, same, precision=lax.Precision.HIGHEST, preferred_element_type=f32)


def vmem_spec():
    return pl.BlockSpec(memory_space=pltpu.VMEM)


def any_spec():
    return pl.BlockSpec(memory_space=pltpu.HBM)


def params(mebibytes):
    return pltpu.CompilerParams(vmem_limit_bytes=mebibytes * 1024 * 1024)


def stats_kernel(own_ref, core_ref, stats_ref, frames_ref):
    core = lax.axis_index("tm") % 2
    frames_ref[core] = own_ref[...]
    frames_ref[1 - core] = core_ref[...]
    width = frames_ref.shape[-1]
    values = [ref[...].astype(f32).reshape(-1, 8, width) for ref in (own_ref, core_ref)]
    mean, square = moments(jnp.concatenate(values, axis=0))
    stats_ref[0:8, :] = jnp.broadcast_to(mean, (8, width))
    stats_ref[8:16, :] = jnp.broadcast_to(square, (8, width))


def chip_stats(own, sibling):
    width = own.shape[-1]
    return pl.pallas_call(
        stats_kernel,
        out_shape=(
            jax.ShapeDtypeStruct((16, width), f32),
            jax.ShapeDtypeStruct((2,) + own.shape, bf16),
        ),
        in_specs=[vmem_spec()] * 2,
        out_specs=(vmem_spec(),) * 2,
        compiler_params=params(10),
        cost_estimate=cost(1.5),
        name="chip_stats",
    )(own, sibling)


def hold_kernel(w_ref, gain_ref, bias_ref, taps_ref, affine_ref, sem):
    copy = pltpu.make_async_copy(w_ref, taps_ref, sem)
    copy.start()
    width = gain_ref.shape[0]
    affine_ref[0:8, :] = jnp.broadcast_to(gain_ref[...].reshape(1, width), (8, width))
    affine_ref[8:16, :] = jnp.broadcast_to(bias_ref[...].reshape(1, width), (8, width))
    copy.wait()


def hold(taps, gain, bias):
    width = gain.shape[0]
    return pl.pallas_call(
        hold_kernel,
        out_shape=(
            jax.ShapeDtypeStruct(taps.shape, bf16),
            jax.ShapeDtypeStruct((16, width), f32),
        ),
        in_specs=[any_spec(), vmem_spec(), vmem_spec()],
        out_specs=(vmem_spec(),) * 2,
        scratch_shapes=[pltpu.SemaphoreType.DMA],
        compiler_params=params(4),
        cost_estimate=cost(1.0),
        name="hold_weights",
    )(taps, gain, bias)


def moments(values):
    count = values.shape[0] * 8 * GROUP_WIDTH
    mean = group_sum(values.sum(axis=0)).sum(axis=0, keepdims=True) / count
    centered = values - mean[None]
    square = group_sum((centered * centered).sum(axis=0)).sum(axis=0, keepdims=True)
    return mean, square


def held_half():
    z = lax.axis_index("mp")
    return (z + z // 2) % 2


def conv_kernel(x_ref, norm_ref, w_ref, keep_ref, send_ref, cols_ref):
    n, frames, rows, cols, width = x_ref.shape
    band = frames * cols
    odd = held_half()
    mean, scale = norm_ref[0:1, :], norm_ref[8:9, :]
    gain, bias = norm_ref[16:17, :], norm_ref[24:25, :]
    column = lax.broadcasted_iota(jnp.int32, (band, width), 0) % cols
    size = keep_ref.shape[0] // n
    for j in range(n):
        cols_ref[j, 0:band, :] = jnp.zeros((band, 3 * width), bf16)
        cols_ref[j, (rows + 1) * band :, :] = jnp.zeros((band, 3 * width), bf16)
        for row in range(rows):
            values = jnp.concatenate([x_ref[j, f, row].astype(f32) for f in range(frames)], axis=0)
            normed = (values - mean) * scale * gain + bias
            hidden = normed / (1.0 + jnp.exp(-normed))
            left = jnp.where(column == 0, 0.0, pltpu.roll(hidden, 1, 0))
            right = jnp.where(column == cols - 1, 0.0, pltpu.roll(hidden, band - 1, 0))
            line = [left.astype(bf16), hidden.astype(bf16), right.astype(bf16)]
            cols_ref[j, (row + 1) * band : (row + 2) * band, :] = jnp.concatenate(line, axis=1)
        total = None
        for tap in range(3):
            window = cols_ref[j, tap * band : (tap + rows) * band, :]
            term = jnp.dot(window, w_ref[tap], preferred_element_type=f32)
            total = term if total is None else total + term
        total = total.reshape(rows, frames, cols, total.shape[-1])
        half = frames // 2
        low = total[:, :half].reshape(size, -1)
        high = total[:, half:].reshape(size, -1)
        here = slice(j * size, (j + 1) * size)

        @pl.when(odd == 0)
        def _():
            keep_ref[here] = low
            send_ref[here] = high.astype(bf16)

        @pl.when(odd == 1)
        def _():
            keep_ref[here] = high
            send_ref[here] = low.astype(bf16)


def pair_conv(pairs, norm, taps, weight):
    n, frames, rows, cols, width = pairs.shape
    width_out = taps.shape[-1]
    count = n * frames * rows * cols // 2
    return pl.pallas_call(
        conv_kernel,
        out_shape=(
            jax.ShapeDtypeStruct((count, width_out), f32),
            jax.ShapeDtypeStruct((count, width_out), bf16),
        ),
        in_specs=[vmem_spec()] * 3,
        out_specs=(vmem_spec(),) * 2,
        scratch_shapes=[pltpu.VMEM((n, (rows + 2) * frames * cols, 3 * width), bf16)],
        compiler_params=params(20),
        cost_estimate=cost(weight),
        name="pair_conv",
    )(pairs, norm, taps)


PAD = 8

CLAIM = {
    "merge": 50.0,
    "conv0": 50.0,
    "collect": 0.0,
    "part": 0.0,
    "part0": 80.0,
    "conv1": 1.0,
    "mine": 50.0,
    "t1": 50.0,
    "g1": 0.0,
    "t2": 0.0,
    "g2": 0.0,
    "g3": 0.0,
    "g4": 50.0,
}


def pair_of(step):
    t = lax.axis_index("tm")
    return (t - t % 2, t - t % 2 + 1, jnp.bitwise_xor(t, 2), jnp.bitwise_xor(t, 3))[step]


def zero_frames(ref, lead, count, rows, width):
    ref[lead + (0,)] = jnp.zeros((rows, width), bf16)
    ref[lead + (count - 1,)] = jnp.zeros((rows, width), bf16)
    for f in range(1, count - 1):
        ref[lead + (f, slice(rows - PAD, rows))] = jnp.zeros((PAD, width), bf16)


def put_pairs(ref, lead, steps, pieces):
    odd = held_half()
    count = ref.shape[-2] - PAD
    steps = list(steps)
    for mine, other in zip(pieces[::2], pieces[1::2], strict=True):
        for j in range(mine.shape[0] // count):
            at = 1 + 2 * pair_of(steps.pop(0))
            ref[lead + (at + odd, slice(0, count))] = mine[j * count : (j + 1) * count]
            ref[lead + (at + 1 - odd, slice(0, count))] = other[j * count : (j + 1) * count]


def grad_kernel(steps, held, extra, *refs):
    cots, pieces, added = refs[:4], refs[4 : 4 + held], refs[4 + held : -3]
    out_ref, s_ref, c_ref = refs[-3:]
    t = lax.axis_index("tm")
    frames, rows, width = s_ref.shape
    zero_frames(s_ref, (), frames, rows, width)
    zero_frames(c_ref, (), frames, rows, c_ref.shape[-1])
    put_pairs(s_ref, (), steps, pieces)
    for block, cot in enumerate(cots):
        first = 1 + 2 * jnp.bitwise_xor(t, block)
        for f in range(2):
            c_ref[first + f, 0 : rows - PAD] = cot[f]
    chip = t // 2 if steps[0] == 0 else 1 - t // 2
    first, length = 1 + 4 * chip, 4
    turned = s_ref[pl.ds(first, length)].reshape(length * rows, width).T
    for k in range(3):
        cot = c_ref[pl.ds(first + 1 - k, length)].reshape(length * rows, -1)
        total = jnp.dot(turned, cot, preferred_element_type=f32)
        if added:
            total = added[0][k] + total
        if extra:
            total = (total + added[1][k]) * 0.5
        out_ref[k] = total


def temporal_grads(steps, cots, pieces, added, weight):
    count, width_out = cots[0].shape[-2:]
    width = pieces[0].shape[-1]
    operands = (*cots, *pieces, *added)
    return pl.pallas_call(
        functools.partial(grad_kernel, steps, len(pieces), len(added) == 2),
        out_shape=jax.ShapeDtypeStruct((3, width, width_out), f32),
        in_specs=[vmem_spec()] * len(operands),
        out_specs=vmem_spec(),
        scratch_shapes=[
            pltpu.VMEM((10, count + PAD, width), bf16),
            pltpu.VMEM((10, count + PAD, width_out), bf16),
        ],
        compiler_params=params(14),
        cost_estimate=cost(weight),
        name="temporal_grads",
    )(*operands)


def temporal_kernel(steps, blocks, *refs):
    *pieces, w_ref, send_ref, keep_ref, s_ref = refs
    frames, rows, width = s_ref.shape
    zero_frames(s_ref, (), frames, rows, width)
    put_pairs(s_ref, (), steps, pieces)
    for i, out in zip(blocks, (send_ref, keep_ref), strict=True):
        first = 2 * jnp.bitwise_xor(lax.axis_index("tm"), i)
        total = None
        for k in range(3):
            window = s_ref[pl.ds(first + k, 2)].reshape(2 * rows, width)
            term = jnp.dot(window, w_ref[k], preferred_element_type=f32)
            total = term if total is None else total + term
        total = total.reshape(2, rows, -1)[:, : rows - PAD]
        out[...] = total.astype(out.dtype)


def temporal_conv(steps, blocks, count, pieces, taps, weight):
    width, width_out = taps.shape[1:]
    return pl.pallas_call(
        functools.partial(temporal_kernel, steps, blocks),
        out_shape=(
            jax.ShapeDtypeStruct((2, count, width_out), bf16),
            jax.ShapeDtypeStruct((2, count, width_out), f32),
        ),
        in_specs=[vmem_spec()] * (len(pieces) + 1),
        out_specs=(vmem_spec(), vmem_spec()),
        scratch_shapes=[pltpu.VMEM((10, count + PAD, width), bf16)],
        compiler_params=params(16),
        cost_estimate=cost(weight),
        name="temporal_conv",
    )(*pieces, taps)


def xor(axis_size, bit):
    return [(i, i ^ bit) for i in range(axis_size)]


def add_kernel(a_ref, b_ref, out_ref):
    out_ref[...] = (a_ref[...].astype(f32) + b_ref[...].astype(f32)).astype(bf16)


def add16(a, b, weight):
    return pl.pallas_call(
        add_kernel,
        out_shape=jax.ShapeDtypeStruct(a.shape, bf16),
        in_specs=[vmem_spec()] * 2,
        out_specs=vmem_spec(),
        compiler_params=params(4),
        cost_estimate=cost(weight),
        name="add_parts",
    )(a, b)


def merge_kernel(s0_ref, s1_ref, affine_ref, out_ref, *, count):
    first, second = s0_ref[0:8, :], s1_ref[0:8, :]
    mean = (first + second) * 0.5
    square = s0_ref[8:16, :] + s1_ref[8:16, :]
    square = square + count * ((first - mean) * (first - mean) + (second - mean) * (second - mean))
    out_ref[0:8, :] = mean
    out_ref[8:16, :] = lax.rsqrt(square / (2.0 * count) + EPSILON)
    out_ref[16:32, :] = affine_ref[...]


def merge_stats(st_own, st_chip, affine, count, weight):
    return pl.pallas_call(
        functools.partial(merge_kernel, count=count),
        out_shape=jax.ShapeDtypeStruct((32, st_own.shape[1]), f32),
        in_specs=[vmem_spec()] * 3,
        out_specs=vmem_spec(),
        compiler_params=params(4),
        cost_estimate=cost(weight),
        name="merge_stats",
    )(st_own, st_chip, affine)


def collect_kernel(a_ref, b_ref, out_ref):
    out_ref[0] = a_ref[...]
    out_ref[1] = b_ref[...]


def collect(a, b, weight):
    return pl.pallas_call(
        collect_kernel,
        out_shape=jax.ShapeDtypeStruct((2,) + a.shape, a.dtype),
        in_specs=[vmem_spec()] * 2,
        out_specs=vmem_spec(),
        compiler_params=params(6),
        cost_estimate=cost(weight),
        name="collect_pairs",
    )(a, b)


def tie(x, *others):
    return lax.optimization_barrier((x,) + others)[0]


def body(activations, norm_gain, norm_bias, spatial_weight, temporal_weight, cotangent):
    own = activations[0]
    frames, rows, cols, width = own.shape
    width_out = spatial_weight.shape[2]
    core, chip = xor(4, 1), xor(4, 2)
    near, across = xor(4, 1), xor(4, 3)
    count = rows * cols
    clips = lax.axis_size("dp")
    pair_clips = clips == 2

    def swap(x):
        return lax.ppermute(x, "dp", [(0, 1), (1, 0)])

    sibling = lax.ppermute(own, "tm", core)
    st_own, pairs = chip_stats(own, sibling)
    st_chip = lax.ppermute(st_own, "tm", chip)
    taps, affine = hold(spatial_weight.reshape(3, 3 * width, width_out), norm_gain, norm_bias)
    raw_chip = lax.ppermute(tie(own, affine), "tm", chip)
    norm = merge_stats(st_own, st_chip, affine, 2 * frames * count * GROUP_WIDTH, CLAIM["merge"])

    keep0, send0 = pair_conv(pairs, norm, taps, CLAIM["conv0"])
    got0 = lax.ppermute(send0, "mp", near)
    raw_chip = tie(raw_chip, keep0)
    raw_both = lax.ppermute(raw_chip, "tm", core)
    far_pairs = collect(raw_chip, raw_both, CLAIM["collect"])
    part0 = add16(keep0, got0, CLAIM["part0"])
    came0 = lax.ppermute(part0, "mp", across)
    keep1, send1 = pair_conv(tie(far_pairs, part0), norm, taps, CLAIM["conv1"])
    got1 = lax.ppermute(send1, "mp", near)
    cot = cotangent.reshape(frames, count, width)
    theirs, far_cot = [], []
    if pair_clips:
        far_cot.append(tie(swap(tie(cot, keep0)), keep1))
    mine0 = add16(tie(part0, keep1, *far_cot), came0, CLAIM["mine"])
    part1 = add16(tie(keep1, mine0), got1, CLAIM["part"])
    came1 = lax.ppermute(part1, "mp", across)
    other0 = lax.ppermute(mine0, "mp", near)
    cot_core = lax.ppermute(tie(cot, mine0), "tm", core)
    cot_chip = lax.ppermute(tie(cot, mine0), "tm", chip)
    if pair_clips:
        theirs.append(swap(mine0))
        far_cot.append(lax.ppermute(tie(far_cot[0], mine0), "tm", core))
        far_cot.append(lax.ppermute(tie(far_cot[0], mine0), "tm", chip))
    mine1 = add16(tie(part1, mine0), came1, CLAIM["mine"])
    other1 = lax.ppermute(tie(mine1, *theirs), "mp", near)
    cots = (cot, cot_core, cot_chip, lax.ppermute(tie(cot_chip, mine1), "tm", core))
    if pair_clips:
        theirs += [swap(tie(other0, mine1)), swap(mine1), swap(other1)]
        far_cot.append(lax.ppermute(tie(far_cot[2], other1), "tm", core))
    grad_own = temporal_grads((0, 1), cots, [tie(mine0, mine1), other0], (), CLAIM["g1"])

    steps = (0, 1, 2, 3)
    pieces = [tie(mine0, grad_own), other0, mine1, other1]
    send, keep_chip = temporal_conv(steps, (3, 2), count, pieces, temporal_weight, CLAIM["t1"])
    far_part = lax.ppermute(send, "tm", core)
    later = [tie(mine0, keep_chip, *theirs[2:3])] + pieces[1:]
    send, keep_own = temporal_conv(steps, (1, 0), count, later, temporal_weight, CLAIM["t2"])
    near_part = lax.ppermute(send, "tm", core)
    to_chip = add16(tie(keep_chip, keep_own), far_part, CLAIM["part"])
    from_chip = lax.ppermute(to_chip, "tm", chip)
    last = [tie(mine1, to_chip), other1]
    grad_own = temporal_grads((2, 3), cots, last, (grad_own,), CLAIM["g3"])
    if pair_clips:
        first = [tie(theirs[0], grad_own), theirs[1]]
        grad_other = temporal_grads((0, 1), far_cot, first, (), CLAIM["g2"])
        last = [tie(theirs[2], grad_other), theirs[3]]
        temporal_grad = temporal_grads((2, 3), far_cot, last, (grad_other, grad_own), CLAIM["g4"])
    else:
        temporal_grad = lax.psum(grad_own, "dp") / clips
    keep_own = tie(keep_own, temporal_grad)
    block = (keep_own + near_part.astype(f32) + from_chip.astype(f32)).astype(bf16)
    return block.reshape(activations.shape), temporal_grad


def solution(mesh):
    in_specs = (
        P("dp", "tm", None, None, "mp"),
        P("mp"),
        P("mp"),
        P(None, "mp", "tm"),
        P(None, "tm", "mp"),
        P("dp", "tm", None, None, "mp"),
    )
    out_specs = (P("dp", "tm", None, None, "mp"), P(None, "tm", "mp"))
    return jax.shard_map(body, mesh=mesh, in_specs=in_specs, out_specs=out_specs, check_vma=False)
```

```python
import functools

import jax
import jax.numpy as jnp
from jax import lax
from jax.experimental import pallas as pl
from jax.experimental.pallas import tpu as pltpu
from jax.sharding import PartitionSpec as P

CHANNELS = 1280
GROUPS = 32
GROUP_WIDTH = CHANNELS // GROUPS
EPSILON = 1e-05


def cost(microseconds):
    return pl.CostEstimate(flops=int(microseconds * 1.15e9), bytes_accessed=1, transcendentals=0)


f32 = jnp.float32
bf16 = jnp.bfloat16


def group_sum(rows):
    width = rows.shape[1]
    first = lax.broadcasted_iota(jnp.int32, (width, width), 0) // GROUP_WIDTH
    second = lax.broadcasted_iota(jnp.int32, (width, width), 1) // GROUP_WIDTH
    same = jnp.where(first == second, 1.0, 0.0).astype(f32)
    return jnp.dot(rows, same, precision=lax.Precision.HIGHEST, preferred_element_type=f32)


def vmem_spec():
    return pl.BlockSpec(memory_space=pltpu.VMEM)


def any_spec():
    return pl.BlockSpec(memory_space=pltpu.HBM)


def params(mebibytes):
    return pltpu.CompilerParams(vmem_limit_bytes=mebibytes * 1024 * 1024)


def stats_kernel(own_ref, core_ref, stats_ref, frames_ref):
    core = lax.axis_index("tm") % 2
    frames_ref[core] = own_ref[...]
    frames_ref[1 - core] = core_ref[...]
    width = frames_ref.shape[-1]
    values = [ref[...].astype(f32).reshape(-1, 8, width) for ref in (own_ref, core_ref)]
    mean, square = moments(jnp.concatenate(values, axis=0))
    stats_ref[0:8, :] = jnp.broadcast_to(mean, (8, width))
    stats_ref[8:16, :] = jnp.broadcast_to(square, (8, width))


def chip_stats(own, sibling):
    width = own.shape[-1]
    return pl.pallas_call(
        stats_kernel,
        out_shape=(
            jax.ShapeDtypeStruct((16, width), f32),
            jax.ShapeDtypeStruct((2,) + own.shape, bf16),
        ),
        in_specs=[vmem_spec()] * 2,
        out_specs=(vmem_spec(),) * 2,
        compiler_params=params(10),
        cost_estimate=cost(1.5),
        name="chip_stats",
    )(own, sibling)


def fetch_kernel(x_ref, out_ref, sem):
    copy = pltpu.make_async_copy(x_ref, out_ref, sem)
    copy.start()
    copy.wait()


def fetch(x, weight):
    return pl.pallas_call(
        fetch_kernel,
        out_shape=jax.ShapeDtypeStruct(x.shape, x.dtype),
        in_specs=[any_spec()],
        out_specs=vmem_spec(),
        scratch_shapes=[pltpu.SemaphoreType.DMA],
        compiler_params=params(2),
        cost_estimate=cost(weight),
        name="fetch",
    )(x)


def hold_kernel(w_ref, gain_ref, bias_ref, taps_ref, affine_ref, sem):
    copy = pltpu.make_async_copy(w_ref, taps_ref, sem)
    copy.start()
    width = gain_ref.shape[0]
    affine_ref[0:8, :] = jnp.broadcast_to(gain_ref[...].reshape(1, width), (8, width))
    affine_ref[8:16, :] = jnp.broadcast_to(bias_ref[...].reshape(1, width), (8, width))
    copy.wait()


def hold(taps, gain, bias):
    width = gain.shape[0]
    return pl.pallas_call(
        hold_kernel,
        out_shape=(
            jax.ShapeDtypeStruct(taps.shape, bf16),
            jax.ShapeDtypeStruct((16, width), f32),
        ),
        in_specs=[any_spec(), vmem_spec(), vmem_spec()],
        out_specs=(vmem_spec(),) * 2,
        scratch_shapes=[pltpu.SemaphoreType.DMA],
        compiler_params=params(4),
        cost_estimate=cost(1.0),
        name="hold_weights",
    )(taps, gain, bias)


def moments(values):
    count = values.shape[0] * 8 * GROUP_WIDTH
    mean = group_sum(values.sum(axis=0)).sum(axis=0, keepdims=True) / count
    centered = values - mean[None]
    square = group_sum((centered * centered).sum(axis=0)).sum(axis=0, keepdims=True)
    return mean, square


def held_half():
    z = lax.axis_index("mp")
    return (z + z // 2) % 2


def conv_kernel(kept, x_ref, norm_ref, w_ref, out_ref, cols_ref):
    pairs, frames, rows, cols, width = x_ref.shape
    band = pairs * cols
    frame = held_half() if kept else 1 - held_half()
    mean, scale = norm_ref[0:1, :], norm_ref[8:9, :]
    gain, bias = norm_ref[16:17, :], norm_ref[24:25, :]
    column = lax.broadcasted_iota(jnp.int32, (band, width), 0) % cols
    cols_ref[0:band, :] = jnp.zeros((band, 3 * width), bf16)
    cols_ref[(rows + 1) * band :, :] = jnp.zeros((band, 3 * width), bf16)
    for row in range(rows):
        values = jnp.concatenate([x_ref[j, frame, row].astype(f32) for j in range(pairs)], axis=0)
        normed = (values - mean) * scale * gain + bias
        hidden = normed / (1.0 + jnp.exp(-normed))
        left = jnp.where(column == 0, 0.0, pltpu.roll(hidden, 1, 0))
        right = jnp.where(column == cols - 1, 0.0, pltpu.roll(hidden, band - 1, 0))
        line = [left.astype(bf16), hidden.astype(bf16), right.astype(bf16)]
        cols_ref[(row + 1) * band : (row + 2) * band, :] = jnp.concatenate(line, axis=1)
    total = None
    for tap in range(3):
        window = cols_ref[tap * band : (tap + rows) * band, :]
        term = jnp.dot(window, w_ref[tap], preferred_element_type=f32)
        total = term if total is None else total + term
    total = total.reshape(rows, pairs, cols, total.shape[-1])
    size = rows * cols
    for j in range(pairs):
        out_ref[j * size : (j + 1) * size] = total[:, j].reshape(size, -1).astype(out_ref.dtype)


def pair_conv(pairs, norm, taps, kept, weight):
    n, frames, rows, cols, width = pairs.shape
    width_out = taps.shape[-1]
    count = n * rows * cols
    return pl.pallas_call(
        functools.partial(conv_kernel, kept),
        out_shape=jax.ShapeDtypeStruct((count, width_out), f32 if kept else bf16),
        in_specs=[vmem_spec()] * 3,
        out_specs=vmem_spec(),
        scratch_shapes=[pltpu.VMEM(((rows + 2) * n * cols, 3 * width), bf16)],
        compiler_params=params(14),
        cost_estimate=cost(weight),
        name="pair_conv",
    )(pairs, norm, taps)


PAD = 8

CLAIM = {
    "fetch": 50.0,
    "merge": 50.0,
    "conv0": 50.0,
    "keep": 0.0,
    "collect": 0.0,
    "part": 0.0,
    "part0": 80.0,
    "conv1": 1.0,
    "mine": 50.0,
    "t1": 50.0,
    "g1": 0.0,
    "t2": 0.0,
    "g2": 0.0,
    "g3": 0.0,
    "g4": 50.0,
}


def pair_of(step):
    t = lax.axis_index("tm")
    return (t - t % 2, t - t % 2 + 1, jnp.bitwise_xor(t, 2), jnp.bitwise_xor(t, 3))[step]


def zero_frames(ref, lead, count, rows, width):
    ref[lead + (0,)] = jnp.zeros((rows, width), bf16)
    ref[lead + (count - 1,)] = jnp.zeros((rows, width), bf16)
    for f in range(1, count - 1):
        ref[lead + (f, slice(rows - PAD, rows))] = jnp.zeros((PAD, width), bf16)


def put_pairs(ref, lead, steps, pieces):
    odd = held_half()
    count = ref.shape[-2] - PAD
    steps = list(steps)
    for mine, other in zip(pieces[::2], pieces[1::2], strict=True):
        for j in range(mine.shape[0] // count):
            at = 1 + 2 * pair_of(steps.pop(0))
            ref[lead + (at + odd, slice(0, count))] = mine[j * count : (j + 1) * count]
            ref[lead + (at + 1 - odd, slice(0, count))] = other[j * count : (j + 1) * count]


def grad_kernel(steps, held, extra, *refs):
    cots, pieces, added = refs[:4], refs[4 : 4 + held], refs[4 + held : -3]
    out_ref, s_ref, c_ref = refs[-3:]
    t = lax.axis_index("tm")
    frames, rows, width = s_ref.shape
    zero_frames(s_ref, (), frames, rows, width)
    zero_frames(c_ref, (), frames, rows, c_ref.shape[-1])
    put_pairs(s_ref, (), steps, pieces)
    for block, cot in enumerate(cots):
        first = 1 + 2 * jnp.bitwise_xor(t, block)
        for f in range(2):
            c_ref[first + f, 0 : rows - PAD] = cot[f]
    chip = t // 2 if steps[0] == 0 else 1 - t // 2
    first, length = 1 + 4 * chip, 4
    turned = s_ref[pl.ds(first, length)].reshape(length * rows, width).T
    for k in range(3):
        cot = c_ref[pl.ds(first + 1 - k, length)].reshape(length * rows, -1)
        total = jnp.dot(turned, cot, preferred_element_type=f32)
        if added:
            total = added[0][k] + total
        if extra:
            total = (total + added[1][k]) * 0.5
        out_ref[k] = total


def temporal_grads(steps, cots, pieces, added, weight):
    count, width_out = cots[0].shape[-2:]
    width = pieces[0].shape[-1]
    operands = (*cots, *pieces, *added)
    return pl.pallas_call(
        functools.partial(grad_kernel, steps, len(pieces), len(added) == 2),
        out_shape=jax.ShapeDtypeStruct((3, width, width_out), f32),
        in_specs=[vmem_spec()] * len(operands),
        out_specs=vmem_spec(),
        scratch_shapes=[
            pltpu.VMEM((10, count + PAD, width), bf16),
            pltpu.VMEM((10, count + PAD, width_out), bf16),
        ],
        compiler_params=params(14),
        cost_estimate=cost(weight),
        name="temporal_grads",
    )(*operands)


def temporal_kernel(steps, blocks, *refs):
    *pieces, w_ref, send_ref, keep_ref, s_ref = refs
    frames, rows, width = s_ref.shape
    zero_frames(s_ref, (), frames, rows, width)
    put_pairs(s_ref, (), steps, pieces)
    for i, out in zip(blocks, (send_ref, keep_ref), strict=True):
        first = 2 * jnp.bitwise_xor(lax.axis_index("tm"), i)
        total = None
        for k in range(3):
            window = s_ref[pl.ds(first + k, 2)].reshape(2 * rows, width)
            term = jnp.dot(window, w_ref[k], preferred_element_type=f32)
            total = term if total is None else total + term
        total = total.reshape(2, rows, -1)[:, : rows - PAD]
        out[...] = total.astype(out.dtype)


def temporal_conv(steps, blocks, count, pieces, taps, weight):
    width, width_out = taps.shape[1:]
    return pl.pallas_call(
        functools.partial(temporal_kernel, steps, blocks),
        out_shape=(
            jax.ShapeDtypeStruct((2, count, width_out), bf16),
            jax.ShapeDtypeStruct((2, count, width_out), f32),
        ),
        in_specs=[vmem_spec()] * (len(pieces) + 1),
        out_specs=(vmem_spec(), vmem_spec()),
        scratch_shapes=[pltpu.VMEM((10, count + PAD, width), bf16)],
        compiler_params=params(16),
        cost_estimate=cost(weight),
        name="temporal_conv",
    )(*pieces, taps)


def xor(axis_size, bit):
    return [(i, i ^ bit) for i in range(axis_size)]


def add_kernel(a_ref, b_ref, out_ref):
    out_ref[...] = (a_ref[...].astype(f32) + b_ref[...].astype(f32)).astype(bf16)


def add16(a, b, weight):
    return pl.pallas_call(
        add_kernel,
        out_shape=jax.ShapeDtypeStruct(a.shape, bf16),
        in_specs=[vmem_spec()] * 2,
        out_specs=vmem_spec(),
        compiler_params=params(4),
        cost_estimate=cost(weight),
        name="add_parts",
    )(a, b)


def merge_kernel(s0_ref, s1_ref, affine_ref, out_ref, *, count):
    first, second = s0_ref[0:8, :], s1_ref[0:8, :]
    mean = (first + second) * 0.5
    square = s0_ref[8:16, :] + s1_ref[8:16, :]
    square = square + count * ((first - mean) * (first - mean) + (second - mean) * (second - mean))
    out_ref[0:8, :] = mean
    out_ref[8:16, :] = lax.rsqrt(square / (2.0 * count) + EPSILON)
    out_ref[16:32, :] = affine_ref[...]


def merge_stats(st_own, st_chip, affine, count, weight):
    return pl.pallas_call(
        functools.partial(merge_kernel, count=count),
        out_shape=jax.ShapeDtypeStruct((32, st_own.shape[1]), f32),
        in_specs=[vmem_spec()] * 3,
        out_specs=vmem_spec(),
        compiler_params=params(4),
        cost_estimate=cost(weight),
        name="merge_stats",
    )(st_own, st_chip, affine)


def collect_kernel(a_ref, b_ref, out_ref):
    out_ref[0] = a_ref[...]
    out_ref[1] = b_ref[...]


def collect(a, b, weight):
    return pl.pallas_call(
        collect_kernel,
        out_shape=jax.ShapeDtypeStruct((2,) + a.shape, a.dtype),
        in_specs=[vmem_spec()] * 2,
        out_specs=vmem_spec(),
        compiler_params=params(6),
        cost_estimate=cost(weight),
        name="collect_pairs",
    )(a, b)


def tie(x, *others):
    return lax.optimization_barrier((x,) + others)[0]


def body(activations, norm_gain, norm_bias, spatial_weight, temporal_weight, cotangent):
    own = activations[0]
    frames, rows, cols, width = own.shape
    width_out = spatial_weight.shape[2]
    core, chip = xor(4, 1), xor(4, 2)
    near, across = xor(4, 1), xor(4, 3)
    count = rows * cols
    clips = lax.axis_size("dp")
    pair_clips = clips == 2

    def swap(x):
        return lax.ppermute(x, "dp", [(0, 1), (1, 0)])

    sibling = lax.ppermute(own, "tm", core)
    st_own, pairs = chip_stats(fetch(own, CLAIM["fetch"]), sibling)
    st_chip = lax.ppermute(st_own, "tm", chip)
    taps, affine = hold(spatial_weight.reshape(3, 3 * width, width_out), norm_gain, norm_bias)
    raw_chip = lax.ppermute(tie(own, affine), "tm", chip)
    norm = merge_stats(st_own, st_chip, affine, 2 * frames * count * GROUP_WIDTH, CLAIM["merge"])

    send0 = pair_conv(pairs, norm, taps, False, CLAIM["conv0"])
    got0 = lax.ppermute(send0, "mp", near)
    keep0 = pair_conv(tie(pairs, send0), norm, taps, True, CLAIM["keep"])
    raw_chip = tie(raw_chip, send0)
    raw_both = lax.ppermute(raw_chip, "tm", core)
    far_pairs = collect(raw_chip, raw_both, CLAIM["collect"])
    part0 = add16(keep0, got0, CLAIM["part0"])
    came0 = lax.ppermute(part0, "mp", across)
    send1 = pair_conv(tie(far_pairs, part0), norm, taps, False, CLAIM["conv1"])
    got1 = lax.ppermute(send1, "mp", near)
    keep1 = pair_conv(tie(far_pairs, send1), norm, taps, True, CLAIM["keep"])
    cot = cotangent.reshape(frames, count, width)
    theirs, far_cot = [], []
    if pair_clips:
        far_cot.append(tie(swap(tie(cot, send0)), send1))
    mine0 = add16(tie(part0, send1, *far_cot), came0, CLAIM["mine"])
    part1 = add16(tie(keep1, mine0), got1, CLAIM["part"])
    came1 = lax.ppermute(part1, "mp", across)
    other0 = lax.ppermute(mine0, "mp", near)
    cot_core = lax.ppermute(tie(cot, mine0), "tm", core)
    cot_chip = lax.ppermute(tie(cot, mine0), "tm", chip)
    if pair_clips:
        theirs.append(swap(mine0))
        far_cot.append(lax.ppermute(tie(far_cot[0], mine0), "tm", core))
        far_cot.append(lax.ppermute(tie(far_cot[0], mine0), "tm", chip))
    mine1 = add16(tie(part1, mine0), came1, CLAIM["mine"])
    other1 = lax.ppermute(tie(mine1, *theirs), "mp", near)
    cots = (cot, cot_core, cot_chip, lax.ppermute(tie(cot_chip, mine1), "tm", core))
    if pair_clips:
        theirs += [swap(tie(other0, mine1)), swap(mine1), swap(other1)]
        far_cot.append(lax.ppermute(tie(far_cot[2], other1), "tm", core))
    grad_own = temporal_grads((0, 1), cots, [tie(mine0, mine1), other0], (), CLAIM["g1"])

    steps = (0, 1, 2, 3)
    pieces = [tie(mine0, grad_own), other0, mine1, other1]
    send, keep_chip = temporal_conv(steps, (3, 2), count, pieces, temporal_weight, CLAIM["t1"])
    far_part = lax.ppermute(send, "tm", core)
    later = [tie(mine0, keep_chip, *theirs[2:3])] + pieces[1:]
    send, keep_own = temporal_conv(steps, (1, 0), count, later, temporal_weight, CLAIM["t2"])
    near_part = lax.ppermute(send, "tm", core)
    to_chip = add16(tie(keep_chip, keep_own), far_part, CLAIM["part"])
    from_chip = lax.ppermute(to_chip, "tm", chip)
    if pair_clips:
        first = [tie(theirs[0], to_chip), theirs[1]]
        grad_other = temporal_grads((0, 1), far_cot, first, (), CLAIM["g2"])
        last = [tie(mine1, grad_other), other1]
        grad_own = temporal_grads((2, 3), cots, last, (grad_own,), CLAIM["g3"])
        last = [tie(theirs[2], grad_own), theirs[3]]
        temporal_grad = temporal_grads((2, 3), far_cot, last, (grad_other, grad_own), CLAIM["g4"])
        keep_own = tie(keep_own, temporal_grad)
    else:
        last = [tie(mine1, to_chip), other1]
        grad_own = temporal_grads((2, 3), cots, last, (grad_own,), CLAIM["g3"])
        temporal_grad = lax.psum(grad_own, "dp") / clips
    block = (keep_own + near_part.astype(f32) + from_chip.astype(f32)).astype(bf16)
    return block.reshape(activations.shape), temporal_grad


def solution(mesh):
    in_specs = (
        P("dp", "tm", None, None, "mp"),
        P("mp"),
        P("mp"),
        P(None, "mp", "tm"),
        P(None, "tm", "mp"),
        P("dp", "tm", None, None, "mp"),
    )
    out_specs = (P("dp", "tm", None, None, "mp"), P(None, "tm", "mp"))
    return jax.shard_map(body, mesh=mesh, in_specs=in_specs, out_specs=out_specs, check_vma=False)
```

```python
import functools

import jax
import jax.numpy as jnp
from jax import lax
from jax.experimental import pallas as pl
from jax.experimental.pallas import tpu as pltpu
from jax.sharding import PartitionSpec as P

CHANNELS = 1280
GROUPS = 32
GROUP_WIDTH = CHANNELS // GROUPS
EPSILON = 1e-05


def cost(microseconds):
    return pl.CostEstimate(flops=int(microseconds * 1.15e9), bytes_accessed=1, transcendentals=0)


f32 = jnp.float32
bf16 = jnp.bfloat16


def group_sum(rows):
    width = rows.shape[1]
    first = lax.broadcasted_iota(jnp.int32, (width, width), 0) // GROUP_WIDTH
    second = lax.broadcasted_iota(jnp.int32, (width, width), 1) // GROUP_WIDTH
    same = jnp.where(first == second, 1.0, 0.0).astype(f32)
    return jnp.dot(rows, same, precision=lax.Precision.HIGHEST, preferred_element_type=f32)


def vmem_spec():
    return pl.BlockSpec(memory_space=pltpu.VMEM)


def any_spec():
    return pl.BlockSpec(memory_space=pltpu.HBM)


def params(mebibytes):
    return pltpu.CompilerParams(vmem_limit_bytes=mebibytes * 1024 * 1024)


def stats_kernel(own_ref, core_ref, stats_ref, frames_ref):
    core = lax.axis_index("tm") % 2
    frames_ref[core] = own_ref[...]
    frames_ref[1 - core] = core_ref[...]
    width = frames_ref.shape[-1]
    values = [ref[...].astype(f32).reshape(-1, 8, width) for ref in (own_ref, core_ref)]
    mean, square = moments(jnp.concatenate(values, axis=0))
    stats_ref[0:8, :] = jnp.broadcast_to(mean, (8, width))
    stats_ref[8:16, :] = jnp.broadcast_to(square, (8, width))


def chip_stats(own, sibling):
    width = own.shape[-1]
    return pl.pallas_call(
        stats_kernel,
        out_shape=(
            jax.ShapeDtypeStruct((16, width), f32),
            jax.ShapeDtypeStruct((2,) + own.shape, bf16),
        ),
        in_specs=[vmem_spec()] * 2,
        out_specs=(vmem_spec(),) * 2,
        compiler_params=params(10),
        cost_estimate=cost(1.5),
        name="chip_stats",
    )(own, sibling)


def fetch_kernel(x_ref, out_ref, sem):
    copy = pltpu.make_async_copy(x_ref, out_ref, sem)
    copy.start()
    copy.wait()


def fetch(x, weight):
    return pl.pallas_call(
        fetch_kernel,
        out_shape=jax.ShapeDtypeStruct(x.shape, x.dtype),
        in_specs=[any_spec()],
        out_specs=vmem_spec(),
        scratch_shapes=[pltpu.SemaphoreType.DMA],
        compiler_params=params(2),
        cost_estimate=cost(weight),
        name="fetch",
    )(x)


def copy_kernel(x_ref, out_ref):
    out_ref[...] = x_ref[...]


def copy(x, weight):
    return pl.pallas_call(
        copy_kernel,
        out_shape=jax.ShapeDtypeStruct(x.shape, x.dtype),
        in_specs=[vmem_spec()],
        out_specs=vmem_spec(),
        compiler_params=params(4),
        cost_estimate=cost(weight),
        name="copy_piece",
    )(x)


def hold_kernel(w_ref, gain_ref, bias_ref, taps_ref, affine_ref, sem):
    copy = pltpu.make_async_copy(w_ref, taps_ref, sem)
    copy.start()
    width = gain_ref.shape[0]
    affine_ref[0:8, :] = jnp.broadcast_to(gain_ref[...].reshape(1, width), (8, width))
    affine_ref[8:16, :] = jnp.broadcast_to(bias_ref[...].reshape(1, width), (8, width))
    copy.wait()


def hold(taps, gain, bias):
    width = gain.shape[0]
    return pl.pallas_call(
        hold_kernel,
        out_shape=(
            jax.ShapeDtypeStruct(taps.shape, bf16),
            jax.ShapeDtypeStruct((16, width), f32),
        ),
        in_specs=[any_spec(), vmem_spec(), vmem_spec()],
        out_specs=(vmem_spec(),) * 2,
        scratch_shapes=[pltpu.SemaphoreType.DMA],
        compiler_params=params(4),
        cost_estimate=cost(1.0),
        name="hold_weights",
    )(taps, gain, bias)


def moments(values):
    count = values.shape[0] * 8 * GROUP_WIDTH
    mean = group_sum(values.sum(axis=0)).sum(axis=0, keepdims=True) / count
    centered = values - mean[None]
    square = group_sum((centered * centered).sum(axis=0)).sum(axis=0, keepdims=True)
    return mean, square


def held_half():
    z = lax.axis_index("mp")
    return (z + z // 2) % 2


def conv_kernel(kept, x_ref, norm_ref, w_ref, out_ref, cols_ref):
    pairs, frames, rows, cols, width = x_ref.shape
    band = pairs * cols
    frame = held_half() if kept else 1 - held_half()
    mean, scale = norm_ref[0:1, :], norm_ref[8:9, :]
    gain, bias = norm_ref[16:17, :], norm_ref[24:25, :]
    column = lax.broadcasted_iota(jnp.int32, (band, width), 0) % cols
    cols_ref[0:band, :] = jnp.zeros((band, 3 * width), bf16)
    cols_ref[(rows + 1) * band :, :] = jnp.zeros((band, 3 * width), bf16)
    for row in range(rows):
        values = jnp.concatenate([x_ref[j, frame, row].astype(f32) for j in range(pairs)], axis=0)
        normed = (values - mean) * scale * gain + bias
        hidden = normed / (1.0 + jnp.exp(-normed))
        left = jnp.where(column == 0, 0.0, pltpu.roll(hidden, 1, 0))
        right = jnp.where(column == cols - 1, 0.0, pltpu.roll(hidden, band - 1, 0))
        line = [left.astype(bf16), hidden.astype(bf16), right.astype(bf16)]
        cols_ref[(row + 1) * band : (row + 2) * band, :] = jnp.concatenate(line, axis=1)
    total = None
    for tap in range(3):
        window = cols_ref[tap * band : (tap + rows) * band, :]
        term = jnp.dot(window, w_ref[tap], preferred_element_type=f32)
        total = term if total is None else total + term
    total = total.reshape(rows, pairs, cols, total.shape[-1])
    size = rows * cols
    for j in range(pairs):
        out_ref[j * size : (j + 1) * size] = total[:, j].reshape(size, -1).astype(out_ref.dtype)


def pair_conv(pairs, norm, taps, kept, weight):
    n, frames, rows, cols, width = pairs.shape
    width_out = taps.shape[-1]
    count = n * rows * cols
    return pl.pallas_call(
        functools.partial(conv_kernel, kept),
        out_shape=jax.ShapeDtypeStruct((count, width_out), f32 if kept else bf16),
        in_specs=[vmem_spec()] * 3,
        out_specs=vmem_spec(),
        scratch_shapes=[pltpu.VMEM(((rows + 2) * n * cols, 3 * width), bf16)],
        compiler_params=params(14),
        cost_estimate=cost(weight),
        name="pair_conv",
    )(pairs, norm, taps)


PAD = 8

CLAIM = {
    "fetch": 50.0,
    "merge": 50.0,
    "conv0": 50.0,
    "keep": 0.0,
    "copy": 1.0,
    "collect": 0.0,
    "part": 0.0,
    "part0": 80.0,
    "conv1": 1.0,
    "mine": 50.0,
    "t1": 50.0,
    "g1": 1.0,
    "t2": 0.0,
    "g2": 0.0,
    "g3": 0.0,
    "g4": 50.0,
}


def pair_of(step):
    t = lax.axis_index("tm")
    return (t - t % 2, t - t % 2 + 1, jnp.bitwise_xor(t, 2), jnp.bitwise_xor(t, 3))[step]


def zero_frames(ref, lead, count, rows, width):
    ref[lead + (0,)] = jnp.zeros((rows, width), bf16)
    ref[lead + (count - 1,)] = jnp.zeros((rows, width), bf16)
    for f in range(1, count - 1):
        ref[lead + (f, slice(rows - PAD, rows))] = jnp.zeros((PAD, width), bf16)


def put_pairs(ref, lead, steps, pieces):
    odd = held_half()
    count = ref.shape[-2] - PAD
    steps = list(steps)
    for mine, other in zip(pieces[::2], pieces[1::2], strict=True):
        for j in range(mine.shape[0] // count):
            at = 1 + 2 * pair_of(steps.pop(0))
            ref[lead + (at + odd, slice(0, count))] = mine[j * count : (j + 1) * count]
            ref[lead + (at + 1 - odd, slice(0, count))] = other[j * count : (j + 1) * count]


def grad_kernel(steps, held, extra, *refs):
    if extra:
        *refs, made_ref, sems = refs
    cots, pieces, added = refs[:4], refs[4 : 4 + held], refs[4 + held : -3]
    out_ref, s_ref, c_ref = refs[-3:]
    t = lax.axis_index("tm")
    frames, rows, width = s_ref.shape
    zero_frames(s_ref, (), frames, rows, width)
    zero_frames(c_ref, (), frames, rows, c_ref.shape[-1])
    put_pairs(s_ref, (), steps, pieces)
    for block, cot in enumerate(cots):
        first = 1 + 2 * jnp.bitwise_xor(t, block)
        for f in range(2):
            c_ref[first + f, 0 : rows - PAD] = cot[f]
    chip = t // 2 if steps[0] == 0 else 1 - t // 2
    first, length = 1 + 4 * chip, 4
    turned = s_ref[pl.ds(first, length)].reshape(length * rows, width).T
    stores = []
    for k in range(3):
        cot = c_ref[pl.ds(first + 1 - k, length)].reshape(length * rows, -1)
        total = jnp.dot(turned, cot, preferred_element_type=f32)
        if extra:
            made_ref[k] = ((added[0][k] + total) + added[1][k]) * 0.5
            stores.append(pltpu.make_async_copy(made_ref.at[k], out_ref.at[k], sems.at[k]))
            stores[k].start()
        elif added:
            out_ref[k] = added[0][k] + total
        else:
            out_ref[k] = total
    for store in stores:
        store.wait()


def temporal_grads(steps, cots, pieces, added, weight):
    count, width_out = cots[0].shape[-2:]
    width = pieces[0].shape[-1]
    extra = len(added) == 2
    operands = (*cots, *pieces, *added)
    scratch = [
        pltpu.VMEM((10, count + PAD, width), bf16),
        pltpu.VMEM((10, count + PAD, width_out), bf16),
    ]
    in_specs = [vmem_spec()] * len(operands)
    if extra:
        scratch += [pltpu.VMEM((3, width, width_out), f32), pltpu.SemaphoreType.DMA((3,))]
    return pl.pallas_call(
        functools.partial(grad_kernel, steps, len(pieces), extra),
        out_shape=jax.ShapeDtypeStruct((3, width, width_out), f32),
        in_specs=in_specs,
        out_specs=any_spec() if extra else vmem_spec(),
        scratch_shapes=scratch,
        compiler_params=params(20 if extra else 14),
        cost_estimate=cost(weight),
        name="temporal_grads",
    )(*operands)


def temporal_kernel(steps, blocks, *refs):
    *refs, s_ref = refs
    pieces, w_ref, outs = refs[: -1 - len(blocks)], refs[-1 - len(blocks)], refs[-len(blocks) :]
    frames, rows, width = s_ref.shape
    zero_frames(s_ref, (), frames, rows, width)
    put_pairs(s_ref, (), steps, pieces)
    for i, out in zip(blocks, outs, strict=True):
        first = 2 * jnp.bitwise_xor(lax.axis_index("tm"), i)
        total = None
        for k in range(3):
            window = s_ref[pl.ds(first + k, 2)].reshape(2 * rows, width)
            term = jnp.dot(window, w_ref[k], preferred_element_type=f32)
            total = term if total is None else total + term
        total = total.reshape(2, rows, -1)[:, : rows - PAD]
        out[...] = total.astype(out.dtype)


def temporal_conv(steps, blocks, types, count, pieces, taps, weight):
    width, width_out = taps.shape[1:]
    return pl.pallas_call(
        functools.partial(temporal_kernel, steps, blocks),
        out_shape=tuple(jax.ShapeDtypeStruct((2, count, width_out), t) for t in types),
        in_specs=[vmem_spec()] * (len(pieces) + 1),
        out_specs=(vmem_spec(),) * len(blocks),
        scratch_shapes=[pltpu.VMEM((10, count + PAD, width), bf16)],
        compiler_params=params(16),
        cost_estimate=cost(weight),
        name="temporal_conv",
    )(*pieces, taps)


def xor(axis_size, bit):
    return [(i, i ^ bit) for i in range(axis_size)]


def add_kernel(a_ref, b_ref, out_ref):
    out_ref[...] = (a_ref[...].astype(f32) + b_ref[...].astype(f32)).astype(bf16)


def add16(a, b, weight):
    return pl.pallas_call(
        add_kernel,
        out_shape=jax.ShapeDtypeStruct(a.shape, bf16),
        in_specs=[vmem_spec()] * 2,
        out_specs=vmem_spec(),
        compiler_params=params(4),
        cost_estimate=cost(weight),
        name="add_parts",
    )(a, b)


def merge_kernel(s0_ref, s1_ref, affine_ref, out_ref, *, count):
    first, second = s0_ref[0:8, :], s1_ref[0:8, :]
    mean = (first + second) * 0.5
    square = s0_ref[8:16, :] + s1_ref[8:16, :]
    square = square + count * ((first - mean) * (first - mean) + (second - mean) * (second - mean))
    out_ref[0:8, :] = mean
    out_ref[8:16, :] = lax.rsqrt(square / (2.0 * count) + EPSILON)
    out_ref[16:32, :] = affine_ref[...]


def merge_stats(st_own, st_chip, affine, count, weight):
    return pl.pallas_call(
        functools.partial(merge_kernel, count=count),
        out_shape=jax.ShapeDtypeStruct((32, st_own.shape[1]), f32),
        in_specs=[vmem_spec()] * 3,
        out_specs=vmem_spec(),
        compiler_params=params(4),
        cost_estimate=cost(weight),
        name="merge_stats",
    )(st_own, st_chip, affine)


def collect_kernel(a_ref, b_ref, out_ref):
    out_ref[0] = a_ref[...]
    out_ref[1] = b_ref[...]


def collect(a, b, weight):
    return pl.pallas_call(
        collect_kernel,
        out_shape=jax.ShapeDtypeStruct((2,) + a.shape, a.dtype),
        in_specs=[vmem_spec()] * 2,
        out_specs=vmem_spec(),
        compiler_params=params(6),
        cost_estimate=cost(weight),
        name="collect_pairs",
    )(a, b)


def tie(x, *others):
    return lax.optimization_barrier((x,) + others)[0]


def body(activations, norm_gain, norm_bias, spatial_weight, temporal_weight, cotangent):
    own = activations[0]
    frames, rows, cols, width = own.shape
    width_out = spatial_weight.shape[2]
    core, chip = xor(4, 1), xor(4, 2)
    near, across = xor(4, 1), xor(4, 3)
    count = rows * cols
    clips = lax.axis_size("dp")
    pair_clips = clips == 2

    def swap(x):
        return lax.ppermute(x, "dp", [(0, 1), (1, 0)])

    sibling = lax.ppermute(own, "tm", core)
    st_own, pairs = chip_stats(fetch(own, CLAIM["fetch"]), sibling)
    st_chip = lax.ppermute(st_own, "tm", chip)
    taps, affine = hold(spatial_weight.reshape(3, 3 * width, width_out), norm_gain, norm_bias)
    raw_chip = lax.ppermute(tie(own, affine), "tm", chip)
    norm = merge_stats(st_own, st_chip, affine, 2 * frames * count * GROUP_WIDTH, CLAIM["merge"])

    send0 = pair_conv(pairs, norm, taps, False, CLAIM["conv0"])
    got0 = lax.ppermute(send0, "mp", near)
    keep0 = pair_conv(tie(pairs, send0), norm, taps, True, CLAIM["keep"])
    raw_chip = tie(raw_chip, send0)
    raw_both = lax.ppermute(raw_chip, "tm", core)
    far_pairs = collect(raw_chip, raw_both, CLAIM["collect"])
    part0 = add16(keep0, got0, CLAIM["part0"])
    came0 = lax.ppermute(part0, "mp", across)
    send1 = pair_conv(tie(far_pairs, part0), norm, taps, False, CLAIM["conv1"])
    got1 = lax.ppermute(send1, "mp", near)
    keep1 = pair_conv(tie(far_pairs, send1), norm, taps, True, CLAIM["keep"])
    cot = cotangent.reshape(frames, count, width)
    theirs, far_cot = [], []
    if pair_clips:
        far_cot.append(tie(swap(tie(cot, send0)), send1))
    mine0 = add16(tie(part0, keep1, *far_cot), came0, CLAIM["mine"])
    part1 = add16(tie(keep1, mine0), got1, CLAIM["part"])
    came1 = lax.ppermute(part1, "mp", across)
    other0 = lax.ppermute(mine0, "mp", near)
    cot_core = lax.ppermute(tie(cot, mine0), "tm", core)
    cot_chip = lax.ppermute(tie(cot, mine0), "tm", chip)
    if pair_clips:
        theirs.append(swap(mine0))
        far_cot.append(lax.ppermute(tie(far_cot[0], mine0), "tm", core))
        far_cot.append(lax.ppermute(tie(far_cot[0], mine0), "tm", chip))
    other0 = copy(other0, CLAIM["copy"])
    mine1 = add16(tie(part1, other0), came1, CLAIM["mine"])
    other1 = lax.ppermute(tie(mine1, *theirs), "mp", near)
    cots = (cot, cot_core, cot_chip, lax.ppermute(tie(cot_chip, other0), "tm", core))
    if pair_clips:
        theirs += [swap(other0), swap(mine1), swap(other1)]
        far_cot.append(lax.ppermute(tie(far_cot[2], other1), "tm", core))
    grad_own = temporal_grads((0, 1), cots, [tie(mine0, mine1, *theirs[1:2]), other0], (), CLAIM["g1"])

    steps = (0, 1, 2, 3)
    pieces = [tie(mine0, grad_own), other0, mine1, other1]
    (send,) = temporal_conv(steps, (3,), (bf16,), count, pieces, temporal_weight, CLAIM["t1"])
    far_part = lax.ppermute(send, "tm", core)
    later = [tie(mine0, send)] + pieces[1:]
    keep_chip, send, keep_own = temporal_conv(
        steps, (2, 1, 0), (f32, bf16, f32), count, later, temporal_weight, CLAIM["t2"]
    )
    near_part = lax.ppermute(send, "tm", core)
    to_chip = add16(tie(keep_chip, *theirs[2:3]), far_part, CLAIM["part"])
    from_chip = lax.ppermute(to_chip, "tm", chip)
    if pair_clips:
        first = [tie(theirs[0], to_chip), theirs[1]]
        grad_other = temporal_grads((0, 1), far_cot, first, (), CLAIM["g2"])
        last = [tie(mine1, grad_other), other1]
        grad_own = temporal_grads((2, 3), cots, last, (grad_own,), CLAIM["g3"])
        last = [tie(theirs[2], grad_own), theirs[3]]
        temporal_grad = temporal_grads((2, 3), far_cot, last, (grad_other, grad_own), CLAIM["g4"])
        keep_own = tie(keep_own, temporal_grad)
    else:
        last = [tie(mine1, to_chip), other1]
        grad_own = temporal_grads((2, 3), cots, last, (grad_own,), CLAIM["g3"])
        temporal_grad = lax.psum(grad_own, "dp") / clips
    block = (keep_own + near_part.astype(f32) + from_chip.astype(f32)).astype(bf16)
    return block.reshape(activations.shape), temporal_grad


def solution(mesh):
    in_specs = (
        P("dp", "tm", None, None, "mp"),
        P("mp"),
        P("mp"),
        P(None, "mp", "tm"),
        P(None, "tm", "mp"),
        P("dp", "tm", None, None, "mp"),
    )
    out_specs = (P("dp", "tm", None, None, "mp"), P(None, "tm", "mp"))
    return jax.shard_map(body, mesh=mesh, in_specs=in_specs, out_specs=out_specs, check_vma=False)
```

```python
import functools

import jax
import jax.numpy as jnp
from jax import lax
from jax.experimental import pallas as pl
from jax.experimental.pallas import tpu as pltpu
from jax.sharding import PartitionSpec as P

CHANNELS = 1280
GROUPS = 32
GROUP_WIDTH = CHANNELS // GROUPS
EPSILON = 1e-05


def cost(microseconds):
    return pl.CostEstimate(flops=int(microseconds * 1.15e9), bytes_accessed=1, transcendentals=0)


f32 = jnp.float32
bf16 = jnp.bfloat16


def group_sum(rows):
    width = rows.shape[1]
    first = lax.broadcasted_iota(jnp.int32, (width, width), 0) // GROUP_WIDTH
    second = lax.broadcasted_iota(jnp.int32, (width, width), 1) // GROUP_WIDTH
    same = jnp.where(first == second, 1.0, 0.0).astype(f32)
    return jnp.dot(rows, same, precision=lax.Precision.HIGHEST, preferred_element_type=f32)


def vmem_spec():
    return pl.BlockSpec(memory_space=pltpu.VMEM)


def any_spec():
    return pl.BlockSpec(memory_space=pltpu.HBM)


def params(mebibytes):
    return pltpu.CompilerParams(vmem_limit_bytes=mebibytes * 1024 * 1024)


def stats_kernel(own_ref, core_ref, stats_ref, frames_ref):
    core = lax.axis_index("tm") % 2
    frames_ref[core] = own_ref[...]
    frames_ref[1 - core] = core_ref[...]
    width = frames_ref.shape[-1]
    values = [ref[...].astype(f32).reshape(-1, 8, width) for ref in (own_ref, core_ref)]
    mean, square = moments(jnp.concatenate(values, axis=0))
    stats_ref[0:8, :] = jnp.broadcast_to(mean, (8, width))
    stats_ref[8:16, :] = jnp.broadcast_to(square, (8, width))


def chip_stats(own, sibling):
    width = own.shape[-1]
    return pl.pallas_call(
        stats_kernel,
        out_shape=(
            jax.ShapeDtypeStruct((16, width), f32),
            jax.ShapeDtypeStruct((2,) + own.shape, bf16),
        ),
        in_specs=[vmem_spec()] * 2,
        out_specs=(vmem_spec(),) * 2,
        compiler_params=params(10),
        cost_estimate=cost(1.5),
        name="chip_stats",
    )(own, sibling)


def fetch_kernel(x_ref, out_ref, sem):
    copy = pltpu.make_async_copy(x_ref, out_ref, sem)
    copy.start()
    copy.wait()


def fetch(x, weight):
    return pl.pallas_call(
        fetch_kernel,
        out_shape=jax.ShapeDtypeStruct(x.shape, x.dtype),
        in_specs=[any_spec()],
        out_specs=vmem_spec(),
        scratch_shapes=[pltpu.SemaphoreType.DMA],
        compiler_params=params(2),
        cost_estimate=cost(weight),
        name="fetch",
    )(x)


def copy_kernel(x_ref, out_ref):
    out_ref[...] = x_ref[...]


def copy(x, weight):
    return pl.pallas_call(
        copy_kernel,
        out_shape=jax.ShapeDtypeStruct(x.shape, x.dtype),
        in_specs=[vmem_spec()],
        out_specs=vmem_spec(),
        compiler_params=params(4),
        cost_estimate=cost(weight),
        name="copy_piece",
    )(x)


def hold_kernel(w_ref, gain_ref, bias_ref, taps_ref, affine_ref, sem):
    copy = pltpu.make_async_copy(w_ref, taps_ref, sem)
    copy.start()
    width = gain_ref.shape[0]
    affine_ref[0:8, :] = jnp.broadcast_to(gain_ref[...].reshape(1, width), (8, width))
    affine_ref[8:16, :] = jnp.broadcast_to(bias_ref[...].reshape(1, width), (8, width))
    copy.wait()


def hold(taps, gain, bias):
    width = gain.shape[0]
    return pl.pallas_call(
        hold_kernel,
        out_shape=(
            jax.ShapeDtypeStruct(taps.shape, bf16),
            jax.ShapeDtypeStruct((16, width), f32),
        ),
        in_specs=[any_spec(), vmem_spec(), vmem_spec()],
        out_specs=(vmem_spec(),) * 2,
        scratch_shapes=[pltpu.SemaphoreType.DMA],
        compiler_params=params(4),
        cost_estimate=cost(1.0),
        name="hold_weights",
    )(taps, gain, bias)


def moments(values):
    count = values.shape[0] * 8 * GROUP_WIDTH
    mean = group_sum(values.sum(axis=0)).sum(axis=0, keepdims=True) / count
    centered = values - mean[None]
    square = group_sum((centered * centered).sum(axis=0)).sum(axis=0, keepdims=True)
    return mean, square


def held_half():
    z = lax.axis_index("mp")
    return (z + z // 2) % 2


def conv_kernel(kept, x_ref, norm_ref, w_ref, out_ref, cols_ref):
    pairs, frames, rows, cols, width = x_ref.shape
    band = pairs * cols
    frame = held_half() if kept else 1 - held_half()
    mean, scale = norm_ref[0:1, :], norm_ref[8:9, :]
    gain, bias = norm_ref[16:17, :], norm_ref[24:25, :]
    column = lax.broadcasted_iota(jnp.int32, (band, width), 0) % cols
    cols_ref[0:band, :] = jnp.zeros((band, 3 * width), bf16)
    cols_ref[(rows + 1) * band :, :] = jnp.zeros((band, 3 * width), bf16)
    for row in range(rows):
        values = jnp.concatenate([x_ref[j, frame, row].astype(f32) for j in range(pairs)], axis=0)
        normed = (values - mean) * scale * gain + bias
        hidden = normed / (1.0 + jnp.exp(-normed))
        left = jnp.where(column == 0, 0.0, pltpu.roll(hidden, 1, 0))
        right = jnp.where(column == cols - 1, 0.0, pltpu.roll(hidden, band - 1, 0))
        line = [left.astype(bf16), hidden.astype(bf16), right.astype(bf16)]
        cols_ref[(row + 1) * band : (row + 2) * band, :] = jnp.concatenate(line, axis=1)
    total = None
    for tap in range(3):
        window = cols_ref[tap * band : (tap + rows) * band, :]
        term = jnp.dot(window, w_ref[tap], preferred_element_type=f32)
        total = term if total is None else total + term
    total = total.reshape(rows, pairs, cols, total.shape[-1])
    size = rows * cols
    for j in range(pairs):
        out_ref[j * size : (j + 1) * size] = total[:, j].reshape(size, -1).astype(out_ref.dtype)


def pair_conv(pairs, norm, taps, kept, weight):
    n, frames, rows, cols, width = pairs.shape
    width_out = taps.shape[-1]
    count = n * rows * cols
    return pl.pallas_call(
        functools.partial(conv_kernel, kept),
        out_shape=jax.ShapeDtypeStruct((count, width_out), f32 if kept else bf16),
        in_specs=[vmem_spec()] * 3,
        out_specs=vmem_spec(),
        scratch_shapes=[pltpu.VMEM(((rows + 2) * n * cols, 3 * width), bf16)],
        compiler_params=params(14),
        cost_estimate=cost(weight),
        name="pair_conv",
    )(pairs, norm, taps)


PAD = 8

CLAIM = {
    "fetch": 50.0,
    "merge": 50.0,
    "conv0": 50.0,
    "keep": 0.0,
    "copy": 1.0,
    "collect": 0.0,
    "part": 0.0,
    "part0": 80.0,
    "conv1": 1.0,
    "mine": 50.0,
    "t1": 50.0,
    "g1": 1.0,
    "t2": 0.0,
    "g2": 0.0,
    "g3": 0.0,
    "g4": 50.0,
}


def pair_of(step):
    t = lax.axis_index("tm")
    return (t - t % 2, t - t % 2 + 1, jnp.bitwise_xor(t, 2), jnp.bitwise_xor(t, 3))[step]


def zero_frames(ref, lead, count, rows, width):
    ref[lead + (0,)] = jnp.zeros((rows, width), bf16)
    ref[lead + (count - 1,)] = jnp.zeros((rows, width), bf16)
    for f in range(1, count - 1):
        ref[lead + (f, slice(rows - PAD, rows))] = jnp.zeros((PAD, width), bf16)


def put_pairs(ref, lead, steps, pieces):
    odd = held_half()
    count = ref.shape[-2] - PAD
    steps = list(steps)
    for mine, other in zip(pieces[::2], pieces[1::2], strict=True):
        for j in range(mine.shape[0] // count):
            at = 1 + 2 * pair_of(steps.pop(0))
            ref[lead + (at + odd, slice(0, count))] = mine[j * count : (j + 1) * count]
            ref[lead + (at + 1 - odd, slice(0, count))] = other[j * count : (j + 1) * count]


def grad_kernel(steps, held, extra, *refs):
    if extra:
        *refs, made_ref, sems = refs
    cots, pieces, added = refs[:4], refs[4 : 4 + held], refs[4 + held : -3]
    out_ref, s_ref, c_ref = refs[-3:]
    t = lax.axis_index("tm")
    frames, rows, width = s_ref.shape
    zero_frames(s_ref, (), frames, rows, width)
    zero_frames(c_ref, (), frames, rows, c_ref.shape[-1])
    put_pairs(s_ref, (), steps, pieces)
    for block, cot in enumerate(cots):
        first = 1 + 2 * jnp.bitwise_xor(t, block)
        for f in range(2):
            c_ref[first + f, 0 : rows - PAD] = cot[f]
    chip = t // 2 if steps[0] == 0 else 1 - t // 2
    first, length = 1 + 4 * chip, 4
    turned = s_ref[pl.ds(first, length)].reshape(length * rows, width).T
    stores = []
    for k in range(3):
        cot = c_ref[pl.ds(first + 1 - k, length)].reshape(length * rows, -1)
        total = jnp.dot(turned, cot, preferred_element_type=f32)
        if extra:
            made_ref[k] = ((added[0][k] + total) + added[1][k]) * 0.5
            stores.append(pltpu.make_async_copy(made_ref.at[k], out_ref.at[k], sems.at[k]))
            stores[k].start()
        elif added:
            out_ref[k] = added[0][k] + total
        else:
            out_ref[k] = total
    for store in stores:
        store.wait()


def temporal_grads(steps, cots, pieces, added, weight):
    count, width_out = cots[0].shape[-2:]
    width = pieces[0].shape[-1]
    extra = len(added) == 2
    operands = (*cots, *pieces, *added)
    scratch = [
        pltpu.VMEM((10, count + PAD, width), bf16),
        pltpu.VMEM((10, count + PAD, width_out), bf16),
    ]
    in_specs = [vmem_spec()] * len(operands)
    if extra:
        scratch += [pltpu.VMEM((3, width, width_out), f32), pltpu.SemaphoreType.DMA((3,))]
    return pl.pallas_call(
        functools.partial(grad_kernel, steps, len(pieces), extra),
        out_shape=jax.ShapeDtypeStruct((3, width, width_out), f32),
        in_specs=in_specs,
        out_specs=any_spec() if extra else vmem_spec(),
        scratch_shapes=scratch,
        compiler_params=params(20 if extra else 14),
        cost_estimate=cost(weight),
        name="temporal_grads",
    )(*operands)


def temporal_kernel(steps, blocks, *refs):
    *refs, s_ref = refs
    pieces, w_ref, outs = refs[: -1 - len(blocks)], refs[-1 - len(blocks)], refs[-len(blocks) :]
    frames, rows, width = s_ref.shape
    zero_frames(s_ref, (), frames, rows, width)
    put_pairs(s_ref, (), steps, pieces)
    for i, out in zip(blocks, outs, strict=True):
        first = 2 * jnp.bitwise_xor(lax.axis_index("tm"), i)
        total = None
        for k in range(3):
            window = s_ref[pl.ds(first + k, 2)].reshape(2 * rows, width)
            term = jnp.dot(window, w_ref[k], preferred_element_type=f32)
            total = term if total is None else total + term
        total = total.reshape(2, rows, -1)[:, : rows - PAD]
        out[...] = total.astype(out.dtype)


def temporal_conv(steps, blocks, types, count, pieces, taps, weight):
    width, width_out = taps.shape[1:]
    return pl.pallas_call(
        functools.partial(temporal_kernel, steps, blocks),
        out_shape=tuple(jax.ShapeDtypeStruct((2, count, width_out), t) for t in types),
        in_specs=[vmem_spec()] * (len(pieces) + 1),
        out_specs=(vmem_spec(),) * len(blocks),
        scratch_shapes=[pltpu.VMEM((10, count + PAD, width), bf16)],
        compiler_params=params(16),
        cost_estimate=cost(weight),
        name="temporal_conv",
    )(*pieces, taps)


def xor(axis_size, bit):
    return [(i, i ^ bit) for i in range(axis_size)]


def add_kernel(a_ref, b_ref, out_ref):
    out_ref[...] = (a_ref[...].astype(f32) + b_ref[...].astype(f32)).astype(bf16)


def add16(a, b, weight):
    return pl.pallas_call(
        add_kernel,
        out_shape=jax.ShapeDtypeStruct(a.shape, bf16),
        in_specs=[vmem_spec()] * 2,
        out_specs=vmem_spec(),
        compiler_params=params(4),
        cost_estimate=cost(weight),
        name="add_parts",
    )(a, b)


def merge_kernel(s0_ref, s1_ref, affine_ref, out_ref, *, count):
    first, second = s0_ref[0:8, :], s1_ref[0:8, :]
    mean = (first + second) * 0.5
    square = s0_ref[8:16, :] + s1_ref[8:16, :]
    square = square + count * ((first - mean) * (first - mean) + (second - mean) * (second - mean))
    out_ref[0:8, :] = mean
    out_ref[8:16, :] = lax.rsqrt(square / (2.0 * count) + EPSILON)
    out_ref[16:32, :] = affine_ref[...]


def merge_stats(st_own, st_chip, affine, count, weight):
    return pl.pallas_call(
        functools.partial(merge_kernel, count=count),
        out_shape=jax.ShapeDtypeStruct((32, st_own.shape[1]), f32),
        in_specs=[vmem_spec()] * 3,
        out_specs=vmem_spec(),
        compiler_params=params(4),
        cost_estimate=cost(weight),
        name="merge_stats",
    )(st_own, st_chip, affine)


def collect_kernel(a_ref, b_ref, out_ref):
    out_ref[0] = a_ref[...]
    out_ref[1] = b_ref[...]


def collect(a, b, weight):
    return pl.pallas_call(
        collect_kernel,
        out_shape=jax.ShapeDtypeStruct((2,) + a.shape, a.dtype),
        in_specs=[vmem_spec()] * 2,
        out_specs=vmem_spec(),
        compiler_params=params(6),
        cost_estimate=cost(weight),
        name="collect_pairs",
    )(a, b)


def tie(x, *others):
    return lax.optimization_barrier((x,) + others)[0]


def body(activations, norm_gain, norm_bias, spatial_weight, temporal_weight, cotangent):
    own = activations[0]
    frames, rows, cols, width = own.shape
    width_out = spatial_weight.shape[2]
    core, chip = xor(4, 1), xor(4, 2)
    near, across = xor(4, 1), xor(4, 3)
    count = rows * cols
    clips = lax.axis_size("dp")
    pair_clips = clips == 2

    def swap(x):
        return lax.ppermute(x, "dp", [(0, 1), (1, 0)])

    sibling = lax.ppermute(own, "tm", core)
    st_own, pairs = chip_stats(fetch(own, CLAIM["fetch"]), sibling)
    st_chip = lax.ppermute(st_own, "tm", chip)
    taps, affine = hold(spatial_weight.reshape(3, 3 * width, width_out), norm_gain, norm_bias)
    raw_chip = lax.ppermute(tie(own, affine), "tm", chip)
    norm = merge_stats(st_own, st_chip, affine, 2 * frames * count * GROUP_WIDTH, CLAIM["merge"])

    send0 = pair_conv(pairs, norm, taps, False, CLAIM["conv0"])
    got0 = lax.ppermute(send0, "mp", near)
    keep0 = pair_conv(tie(pairs, send0), norm, taps, True, CLAIM["keep"])
    raw_chip = tie(raw_chip, send0)
    raw_both = lax.ppermute(raw_chip, "tm", core)
    far_pairs = collect(raw_chip, raw_both, CLAIM["collect"])
    part0 = add16(keep0, got0, CLAIM["part0"])
    came0 = lax.ppermute(part0, "mp", across)
    send1 = pair_conv(tie(far_pairs, part0), norm, taps, False, CLAIM["conv1"])
    got1 = lax.ppermute(send1, "mp", near)
    keep1 = pair_conv(tie(far_pairs, send1), norm, taps, True, CLAIM["keep"])
    cot = cotangent.reshape(frames, count, width)
    theirs, far_cot = [], []
    if pair_clips:
        far_cot.append(tie(swap(tie(cot, send0)), send1))
    mine0 = add16(tie(part0, keep1, *far_cot), came0, CLAIM["mine"])
    part1 = add16(tie(keep1, mine0), got1, CLAIM["part"])
    came1 = lax.ppermute(part1, "mp", across)
    other0 = lax.ppermute(mine0, "mp", near)
    cot_core = lax.ppermute(tie(cot, mine0), "tm", core)
    cot_chip = lax.ppermute(tie(cot, mine0), "tm", chip)
    if pair_clips:
        theirs.append(swap(mine0))
        far_cot.append(lax.ppermute(tie(far_cot[0], mine0), "tm", core))
        far_cot.append(lax.ppermute(tie(far_cot[0], mine0), "tm", chip))
    other0 = copy(tie(other0, *theirs), CLAIM["copy"])
    mine1 = add16(tie(part1, other0), came1, CLAIM["mine"])
    other1 = lax.ppermute(mine1, "mp", near)
    cots = (cot, cot_core, cot_chip, lax.ppermute(tie(cot_chip, other0), "tm", core))
    if pair_clips:
        theirs += [swap(other0), swap(mine1), swap(other1)]
        far_cot.append(lax.ppermute(tie(far_cot[2], other1), "tm", core))
    grad_own = temporal_grads((0, 1), cots, [tie(mine0, mine1, *theirs[1:2]), other0], (), CLAIM["g1"])

    steps = (0, 1, 2, 3)
    pieces = [tie(mine0, grad_own), other0, mine1, other1]
    (send,) = temporal_conv(steps, (3,), (bf16,), count, pieces, temporal_weight, CLAIM["t1"])
    far_part = lax.ppermute(send, "tm", core)
    later = [tie(mine0, send)] + pieces[1:]
    (keep_chip,) = temporal_conv(steps, (2,), (f32,), count, later, temporal_weight, CLAIM["t2"])
    to_chip = add16(tie(keep_chip, *theirs[2:3]), far_part, CLAIM["part"])
    later = [tie(mine0, to_chip)] + pieces[1:]
    send, keep_own = temporal_conv(steps, (1, 0), (bf16, f32), count, later, temporal_weight, CLAIM["t2"])
    near_part = lax.ppermute(send, "tm", core)
    from_chip = lax.ppermute(to_chip, "tm", chip)
    if pair_clips:
        first = [tie(theirs[0], to_chip), theirs[1]]
        grad_other = temporal_grads((0, 1), far_cot, first, (), CLAIM["g2"])
        last = [tie(mine1, grad_other), other1]
        grad_own = temporal_grads((2, 3), cots, last, (grad_own,), CLAIM["g3"])
        last = [tie(theirs[2], grad_own), theirs[3]]
        temporal_grad = temporal_grads((2, 3), far_cot, last, (grad_other, grad_own), CLAIM["g4"])
        keep_own = tie(keep_own, temporal_grad)
    else:
        last = [tie(mine1, to_chip), other1]
        grad_own = temporal_grads((2, 3), cots, last, (grad_own,), CLAIM["g3"])
        temporal_grad = lax.psum(grad_own, "dp") / clips
    block = (keep_own + near_part.astype(f32) + from_chip.astype(f32)).astype(bf16)
    return block.reshape(activations.shape), temporal_grad


def solution(mesh):
    in_specs = (
        P("dp", "tm", None, None, "mp"),
        P("mp"),
        P("mp"),
        P(None, "mp", "tm"),
        P(None, "tm", "mp"),
        P("dp", "tm", None, None, "mp"),
    )
    out_specs = (P("dp", "tm", None, None, "mp"), P(None, "tm", "mp"))
    return jax.shard_map(body, mesh=mesh, in_specs=in_specs, out_specs=out_specs, check_vma=False)
```

```python
import functools

import jax
import jax.numpy as jnp
from jax import lax
from jax.experimental import pallas as pl
from jax.experimental.pallas import tpu as pltpu
from jax.sharding import PartitionSpec as P

CHANNELS = 1280
GROUPS = 32
GROUP_WIDTH = CHANNELS // GROUPS
EPSILON = 1e-05


def cost(microseconds):
    return pl.CostEstimate(flops=int(microseconds * 1.15e9), bytes_accessed=1, transcendentals=0)


f32 = jnp.float32
bf16 = jnp.bfloat16


def group_sum(rows):
    width = rows.shape[1]
    first = lax.broadcasted_iota(jnp.int32, (width, width), 0) // GROUP_WIDTH
    second = lax.broadcasted_iota(jnp.int32, (width, width), 1) // GROUP_WIDTH
    same = jnp.where(first == second, 1.0, 0.0).astype(f32)
    return jnp.dot(rows, same, precision=lax.Precision.HIGHEST, preferred_element_type=f32)


def vmem_spec():
    return pl.BlockSpec(memory_space=pltpu.VMEM)


def any_spec():
    return pl.BlockSpec(memory_space=pltpu.HBM)


def params(mebibytes):
    return pltpu.CompilerParams(vmem_limit_bytes=mebibytes * 1024 * 1024)


def stats_kernel(own_ref, core_ref, stats_ref, frames_ref):
    core = lax.axis_index("tm") % 2
    frames_ref[core] = own_ref[...]
    frames_ref[1 - core] = core_ref[...]
    width = frames_ref.shape[-1]
    values = [ref[...].astype(f32).reshape(-1, 8, width) for ref in (own_ref, core_ref)]
    mean, square = moments(jnp.concatenate(values, axis=0))
    stats_ref[0:8, :] = jnp.broadcast_to(mean, (8, width))
    stats_ref[8:16, :] = jnp.broadcast_to(square, (8, width))


def chip_stats(own, sibling):
    width = own.shape[-1]
    return pl.pallas_call(
        stats_kernel,
        out_shape=(
            jax.ShapeDtypeStruct((16, width), f32),
            jax.ShapeDtypeStruct((2,) + own.shape, bf16),
        ),
        in_specs=[vmem_spec()] * 2,
        out_specs=(vmem_spec(),) * 2,
        compiler_params=params(10),
        cost_estimate=cost(1.5),
        name="chip_stats",
    )(own, sibling)


def fetch_kernel(x_ref, out_ref, sem):
    copy = pltpu.make_async_copy(x_ref, out_ref, sem)
    copy.start()
    copy.wait()


def fetch(x, weight):
    return pl.pallas_call(
        fetch_kernel,
        out_shape=jax.ShapeDtypeStruct(x.shape, x.dtype),
        in_specs=[any_spec()],
        out_specs=vmem_spec(),
        scratch_shapes=[pltpu.SemaphoreType.DMA],
        compiler_params=params(2),
        cost_estimate=cost(weight),
        name="fetch",
    )(x)


def copy_kernel(x_ref, out_ref):
    out_ref[...] = x_ref[...]


def copy(x, weight):
    return pl.pallas_call(
        copy_kernel,
        out_shape=jax.ShapeDtypeStruct(x.shape, x.dtype),
        in_specs=[vmem_spec()],
        out_specs=vmem_spec(),
        compiler_params=params(4),
        cost_estimate=cost(weight),
        name="copy_piece",
    )(x)


def hold_kernel(w_ref, gain_ref, bias_ref, taps_ref, affine_ref, sem):
    copy = pltpu.make_async_copy(w_ref, taps_ref, sem)
    copy.start()
    width = gain_ref.shape[0]
    affine_ref[0:8, :] = jnp.broadcast_to(gain_ref[...].reshape(1, width), (8, width))
    affine_ref[8:16, :] = jnp.broadcast_to(bias_ref[...].reshape(1, width), (8, width))
    copy.wait()


def hold(taps, gain, bias):
    width = gain.shape[0]
    return pl.pallas_call(
        hold_kernel,
        out_shape=(
            jax.ShapeDtypeStruct(taps.shape, bf16),
            jax.ShapeDtypeStruct((16, width), f32),
        ),
        in_specs=[any_spec(), vmem_spec(), vmem_spec()],
        out_specs=(vmem_spec(),) * 2,
        scratch_shapes=[pltpu.SemaphoreType.DMA],
        compiler_params=params(4),
        cost_estimate=cost(1.0),
        name="hold_weights",
    )(taps, gain, bias)


def moments(values):
    count = values.shape[0] * 8 * GROUP_WIDTH
    mean = group_sum(values.sum(axis=0)).sum(axis=0, keepdims=True) / count
    centered = values - mean[None]
    square = group_sum((centered * centered).sum(axis=0)).sum(axis=0, keepdims=True)
    return mean, square


def held_half():
    z = lax.axis_index("mp")
    return (z + z // 2) % 2


def conv_kernel(kept, x_ref, norm_ref, w_ref, out_ref, cols_ref):
    pairs, frames, rows, cols, width = x_ref.shape
    band = pairs * cols
    frame = held_half() if kept else 1 - held_half()
    mean, scale = norm_ref[0:1, :], norm_ref[8:9, :]
    gain, bias = norm_ref[16:17, :], norm_ref[24:25, :]
    column = lax.broadcasted_iota(jnp.int32, (band, width), 0) % cols
    cols_ref[0:band, :] = jnp.zeros((band, 3 * width), bf16)
    cols_ref[(rows + 1) * band :, :] = jnp.zeros((band, 3 * width), bf16)
    for row in range(rows):
        values = jnp.concatenate([x_ref[j, frame, row].astype(f32) for j in range(pairs)], axis=0)
        normed = (values - mean) * scale * gain + bias
        hidden = normed / (1.0 + jnp.exp(-normed))
        left = jnp.where(column == 0, 0.0, pltpu.roll(hidden, 1, 0))
        right = jnp.where(column == cols - 1, 0.0, pltpu.roll(hidden, band - 1, 0))
        line = [left.astype(bf16), hidden.astype(bf16), right.astype(bf16)]
        cols_ref[(row + 1) * band : (row + 2) * band, :] = jnp.concatenate(line, axis=1)
    total = None
    for tap in range(3):
        window = cols_ref[tap * band : (tap + rows) * band, :]
        term = jnp.dot(window, w_ref[tap], preferred_element_type=f32)
        total = term if total is None else total + term
    total = total.reshape(rows, pairs, cols, total.shape[-1])
    size = rows * cols
    for j in range(pairs):
        out_ref[j * size : (j + 1) * size] = total[:, j].reshape(size, -1).astype(out_ref.dtype)


def pair_conv(pairs, norm, taps, kept, weight):
    n, frames, rows, cols, width = pairs.shape
    width_out = taps.shape[-1]
    count = n * rows * cols
    return pl.pallas_call(
        functools.partial(conv_kernel, kept),
        out_shape=jax.ShapeDtypeStruct((count, width_out), f32 if kept else bf16),
        in_specs=[vmem_spec()] * 3,
        out_specs=vmem_spec(),
        scratch_shapes=[pltpu.VMEM(((rows + 2) * n * cols, 3 * width), bf16)],
        compiler_params=params(14),
        cost_estimate=cost(weight),
        name="pair_conv",
    )(pairs, norm, taps)


PAD = 8

CLAIM = {
    "fetch": 50.0,
    "merge": 50.0,
    "conv0": 50.0,
    "keep": 0.0,
    "copy": 1.0,
    "collect": 0.0,
    "part": 0.0,
    "part0": 80.0,
    "conv1": 1.0,
    "mine": 50.0,
    "t1": 50.0,
    "g1": 1.0,
    "t2": 0.0,
    "g2": 0.0,
    "g3": 0.0,
    "g4": 50.0,
}


def pair_of(step):
    t = lax.axis_index("tm")
    return (t - t % 2, t - t % 2 + 1, jnp.bitwise_xor(t, 2), jnp.bitwise_xor(t, 3))[step]


def zero_frames(ref, lead, count, rows, width):
    ref[lead + (0,)] = jnp.zeros((rows, width), bf16)
    ref[lead + (count - 1,)] = jnp.zeros((rows, width), bf16)
    for f in range(1, count - 1):
        ref[lead + (f, slice(rows - PAD, rows))] = jnp.zeros((PAD, width), bf16)


def put_pairs(ref, lead, steps, pieces):
    odd = held_half()
    count = ref.shape[-2] - PAD
    steps = list(steps)
    for mine, other in zip(pieces[::2], pieces[1::2], strict=True):
        for j in range(mine.shape[0] // count):
            at = 1 + 2 * pair_of(steps.pop(0))
            ref[lead + (at + odd, slice(0, count))] = mine[j * count : (j + 1) * count]
            ref[lead + (at + 1 - odd, slice(0, count))] = other[j * count : (j + 1) * count]


def grad_kernel(steps, held, extra, *refs):
    if extra:
        *refs, made_ref, sems = refs
    cots, pieces, added = refs[:4], refs[4 : 4 + held], refs[4 + held : -3]
    out_ref, s_ref, c_ref = refs[-3:]
    t = lax.axis_index("tm")
    frames, rows, width = s_ref.shape
    for f in range(1, frames - 1):
        s_ref[f, rows - PAD :] = jnp.zeros((PAD, width), bf16)
    zero_frames(c_ref, (), frames, rows, c_ref.shape[-1])
    put_pairs(s_ref, (), steps, pieces)
    for block, cot in enumerate(cots):
        first = 1 + 2 * jnp.bitwise_xor(t, block)
        for f in range(2):
            c_ref[first + f, 0 : rows - PAD] = cot[f]
    chip = t // 2 if steps[0] == 0 else 1 - t // 2
    first, length = 1 + 4 * chip, 4
    turned = s_ref[pl.ds(first, length)].reshape(length * rows, width).T
    stores = []
    for k in range(3):
        cot = c_ref[pl.ds(first + 1 - k, length)].reshape(length * rows, -1)
        total = jnp.dot(turned, cot, preferred_element_type=f32)
        if extra:
            made_ref[k] = ((added[0][k] + total) + added[1][k]) * 0.5
            stores.append(pltpu.make_async_copy(made_ref.at[k], out_ref.at[k], sems.at[k]))
            stores[k].start()
        elif added:
            out_ref[k] = added[0][k] + total
        else:
            out_ref[k] = total
    for store in stores:
        store.wait()


def temporal_grads(steps, cots, pieces, added, weight):
    count, width_out = cots[0].shape[-2:]
    width = pieces[0].shape[-1]
    extra = len(added) == 2
    operands = (*cots, *pieces, *added)
    scratch = [
        pltpu.VMEM((10, count + PAD, width), bf16),
        pltpu.VMEM((10, count + PAD, width_out), bf16),
    ]
    in_specs = [vmem_spec()] * len(operands)
    if extra:
        scratch += [pltpu.VMEM((3, width, width_out), f32), pltpu.SemaphoreType.DMA((3,))]
    return pl.pallas_call(
        functools.partial(grad_kernel, steps, len(pieces), extra),
        out_shape=jax.ShapeDtypeStruct((3, width, width_out), f32),
        in_specs=in_specs,
        out_specs=any_spec() if extra else vmem_spec(),
        scratch_shapes=scratch,
        compiler_params=params(20 if extra else 14),
        cost_estimate=cost(weight),
        name="temporal_grads",
    )(*operands)


def temporal_kernel(steps, blocks, *refs):
    *refs, s_ref = refs
    pieces, w_ref, outs = refs[: -1 - len(blocks)], refs[-1 - len(blocks)], refs[-len(blocks) :]
    frames, rows, width = s_ref.shape
    s_ref[0] = jnp.zeros((rows, width), bf16)
    s_ref[frames - 1] = jnp.zeros((rows, width), bf16)
    put_pairs(s_ref, (), steps, pieces)
    for i, out in zip(blocks, outs, strict=True):
        first = 2 * jnp.bitwise_xor(lax.axis_index("tm"), i)
        total = None
        for k in range(3):
            window = s_ref[pl.ds(first + k, 2)].reshape(2 * rows, width)
            term = jnp.dot(window, w_ref[k], preferred_element_type=f32)
            total = term if total is None else total + term
        total = total.reshape(2, rows, -1)[:, : rows - PAD]
        out[...] = total.astype(out.dtype)


def temporal_conv(steps, blocks, types, count, pieces, taps, weight):
    width, width_out = taps.shape[1:]
    return pl.pallas_call(
        functools.partial(temporal_kernel, steps, blocks),
        out_shape=tuple(jax.ShapeDtypeStruct((2, count, width_out), t) for t in types),
        in_specs=[vmem_spec()] * (len(pieces) + 1),
        out_specs=(vmem_spec(),) * len(blocks),
        scratch_shapes=[pltpu.VMEM((10, count + PAD, width), bf16)],
        compiler_params=params(16),
        cost_estimate=cost(weight),
        name="temporal_conv",
    )(*pieces, taps)


def xor(axis_size, bit):
    return [(i, i ^ bit) for i in range(axis_size)]


def add_kernel(a_ref, b_ref, out_ref):
    out_ref[...] = (a_ref[...].astype(f32) + b_ref[...].astype(f32)).astype(bf16)


def add16(a, b, weight):
    return pl.pallas_call(
        add_kernel,
        out_shape=jax.ShapeDtypeStruct(a.shape, bf16),
        in_specs=[vmem_spec()] * 2,
        out_specs=vmem_spec(),
        compiler_params=params(4),
        cost_estimate=cost(weight),
        name="add_parts",
    )(a, b)


def merge_kernel(s0_ref, s1_ref, affine_ref, out_ref, *, count):
    first, second = s0_ref[0:8, :], s1_ref[0:8, :]
    mean = (first + second) * 0.5
    square = s0_ref[8:16, :] + s1_ref[8:16, :]
    square = square + count * ((first - mean) * (first - mean) + (second - mean) * (second - mean))
    out_ref[0:8, :] = mean
    out_ref[8:16, :] = lax.rsqrt(square / (2.0 * count) + EPSILON)
    out_ref[16:32, :] = affine_ref[...]


def merge_stats(st_own, st_chip, affine, count, weight):
    return pl.pallas_call(
        functools.partial(merge_kernel, count=count),
        out_shape=jax.ShapeDtypeStruct((32, st_own.shape[1]), f32),
        in_specs=[vmem_spec()] * 3,
        out_specs=vmem_spec(),
        compiler_params=params(4),
        cost_estimate=cost(weight),
        name="merge_stats",
    )(st_own, st_chip, affine)


def collect_kernel(a_ref, b_ref, out_ref):
    out_ref[0] = a_ref[...]
    out_ref[1] = b_ref[...]


def collect(a, b, weight):
    return pl.pallas_call(
        collect_kernel,
        out_shape=jax.ShapeDtypeStruct((2,) + a.shape, a.dtype),
        in_specs=[vmem_spec()] * 2,
        out_specs=vmem_spec(),
        compiler_params=params(6),
        cost_estimate=cost(weight),
        name="collect_pairs",
    )(a, b)


def tie(x, *others):
    return lax.optimization_barrier((x,) + others)[0]


def body(activations, norm_gain, norm_bias, spatial_weight, temporal_weight, cotangent):
    own = activations[0]
    frames, rows, cols, width = own.shape
    width_out = spatial_weight.shape[2]
    core, chip = xor(4, 1), xor(4, 2)
    near, across = xor(4, 1), xor(4, 3)
    count = rows * cols
    clips = lax.axis_size("dp")
    pair_clips = clips == 2

    def swap(x):
        return lax.ppermute(x, "dp", [(0, 1), (1, 0)])

    sibling = lax.ppermute(own, "tm", core)
    st_own, pairs = chip_stats(fetch(own, CLAIM["fetch"]), sibling)
    st_chip = lax.ppermute(st_own, "tm", chip)
    taps, affine = hold(spatial_weight.reshape(3, 3 * width, width_out), norm_gain, norm_bias)
    raw_chip = lax.ppermute(tie(own, affine), "tm", chip)
    norm = merge_stats(st_own, st_chip, affine, 2 * frames * count * GROUP_WIDTH, CLAIM["merge"])

    send0 = pair_conv(pairs, norm, taps, False, CLAIM["conv0"])
    got0 = lax.ppermute(send0, "mp", near)
    keep0 = pair_conv(tie(pairs, send0), norm, taps, True, CLAIM["keep"])
    raw_chip = tie(raw_chip, send0)
    raw_both = lax.ppermute(raw_chip, "tm", core)
    far_pairs = collect(raw_chip, raw_both, CLAIM["collect"])
    part0 = add16(keep0, got0, CLAIM["part0"])
    came0 = lax.ppermute(part0, "mp", across)
    send1 = pair_conv(tie(far_pairs, part0), norm, taps, False, CLAIM["conv1"])
    got1 = lax.ppermute(send1, "mp", near)
    keep1 = pair_conv(tie(far_pairs, send1), norm, taps, True, CLAIM["keep"])
    cot = cotangent.reshape(frames, count, width)
    theirs, far_cot = [], []
    if pair_clips:
        far_cot.append(tie(swap(tie(cot, send0)), send1))
    mine0 = add16(tie(part0, keep1, *far_cot), came0, CLAIM["mine"])
    part1 = add16(tie(keep1, mine0), got1, CLAIM["part"])
    came1 = lax.ppermute(part1, "mp", across)
    other0 = lax.ppermute(mine0, "mp", near)
    cot_core = lax.ppermute(tie(cot, mine0), "tm", core)
    cot_chip = lax.ppermute(tie(cot, mine0), "tm", chip)
    if pair_clips:
        theirs.append(swap(mine0))
        far_cot.append(lax.ppermute(tie(far_cot[0], mine0), "tm", core))
        far_cot.append(lax.ppermute(tie(far_cot[0], mine0), "tm", chip))
    other0 = copy(tie(other0, *theirs), CLAIM["copy"])
    mine1 = add16(tie(part1, other0), came1, CLAIM["mine"])
    other1 = lax.ppermute(mine1, "mp", near)
    cots = (cot, cot_core, cot_chip, lax.ppermute(tie(cot_chip, other0), "tm", core))
    if pair_clips:
        theirs += [swap(other0), swap(mine1), swap(other1)]
        far_cot.append(lax.ppermute(tie(far_cot[2], other1), "tm", core))
    grad_own = temporal_grads((0, 1), cots, [tie(mine0, mine1, *theirs[1:2]), other0], (), CLAIM["g1"])

    steps = (0, 1, 2, 3)
    pieces = [tie(mine0, grad_own), other0, mine1, other1]
    (send,) = temporal_conv(steps, (3,), (bf16,), count, pieces, temporal_weight, CLAIM["t1"])
    far_part = lax.ppermute(send, "tm", core)
    later = [tie(mine0, send)] + pieces[1:]
    (keep_chip,) = temporal_conv(steps, (2,), (f32,), count, later, temporal_weight, CLAIM["t2"])
    to_chip = add16(tie(keep_chip, *theirs[2:3]), far_part, CLAIM["part"])
    later = [tie(mine0, to_chip)] + pieces[1:]
    send, keep_own = temporal_conv(steps, (1, 0), (bf16, f32), count, later, temporal_weight, CLAIM["t2"])
    near_part = lax.ppermute(send, "tm", core)
    from_chip = lax.ppermute(to_chip, "tm", chip)
    if pair_clips:
        first = [tie(theirs[0], to_chip), theirs[1]]
        grad_other = temporal_grads((0, 1), far_cot, first, (), CLAIM["g2"])
        last = [tie(mine1, grad_other), other1]
        grad_own = temporal_grads((2, 3), cots, last, (grad_own,), CLAIM["g3"])
        last = [tie(theirs[2], grad_own), theirs[3]]
        temporal_grad = temporal_grads((2, 3), far_cot, last, (grad_other, grad_own), CLAIM["g4"])
        keep_own = tie(keep_own, temporal_grad)
    else:
        last = [tie(mine1, to_chip), other1]
        grad_own = temporal_grads((2, 3), cots, last, (grad_own,), CLAIM["g3"])
        temporal_grad = lax.psum(grad_own, "dp") / clips
    block = (keep_own + near_part.astype(f32) + from_chip.astype(f32)).astype(bf16)
    return block.reshape(activations.shape), temporal_grad


def solution(mesh):
    in_specs = (
        P("dp", "tm", None, None, "mp"),
        P("mp"),
        P("mp"),
        P(None, "mp", "tm"),
        P(None, "tm", "mp"),
        P("dp", "tm", None, None, "mp"),
    )
    out_specs = (P("dp", "tm", None, None, "mp"), P(None, "tm", "mp"))
    return jax.shard_map(body, mesh=mesh, in_specs=in_specs, out_specs=out_specs, check_vma=False)
```
